256 devices in a mesh: prod: 32 (over y, z), week: 8 (over x, core).
Axes of the slice: x: 4, y: 4, z: 8, core: 2. Of those that a mesh axis runs over, the one named last changes fastest.
Arguments:
- regressors: bfloat16 [32, 512, 49152], P(None, 'week', 'prod')
- weights: int32 [512, 49152], P('week', 'prod'), may hold values from 1 to 4
- first_week: int32 [49152], P('prod'), may hold values from 0 to 511, as said below
- last_week: int32 [49152], P('prod'), may hold values from 0 to 511, as said below
Outputs:
- demeaned: bfloat16 [32, 512, 49152], P(None, 'week', 'prod')
- gram: float32 [32, 32], replicated
The draws below stay inside these ranges and needn't reach their ends.
Inputs may be any that keep to these rules, and one draw needn't show every extreme that they name: `first_week`: product 0 is active in every week, product 1 only in week 0, the last product only in week 512 - 1. last_week[p] >= first_week[p] for every product p.
All inputs are finite; a program needn't handle non-finite values.
Results may differ from the reference program's by a relative error of at most 0.001.
Values sent between devices are 32-bit elements; how exact they have to be, the bound alone decides.
A program may use at most 128 MiB of HBM per device.

```python
import jax
import jax.numpy as jnp
from jax import lax

K = 32
WEEKS = 512
SWEEPS = 4
P_DEV = 1536
PRODUCTS = 49152


def lifetimes(key):
    key_start, key_span = jax.random.split(key)
    start = jax.random.randint(key_start, (PRODUCTS,), 0, WEEKS)
    span = jax.random.randint(key_span, (PRODUCTS,), 1, WEEKS + 1)
    finish = jnp.minimum(start + span - 1, WEEKS - 1)
    index = jnp.arange(PRODUCTS)
    start = jnp.where(index == 0, 0, start)
    finish = jnp.where(index == 0, WEEKS - 1, finish)
    start = jnp.where(index == 1, 0, start)
    finish = jnp.where(index == 1, 0, finish)
    start = jnp.where(index == PRODUCTS - 1, WEEKS - 1, start)
    finish = jnp.where(index == PRODUCTS - 1, WEEKS - 1, finish)
    return (start.astype(jnp.int32), finish.astype(jnp.int32))


def draw_first_week(key, part):
    return lifetimes(key)[0]


def draw_last_week(key, part):
    return lifetimes(key)[1]


def draw_regressors(key, part):
    key = jax.random.fold_in(key, 11)
    key_noise, key_week, key_prod = jax.random.split(key, 3)
    noise = jax.random.normal(key_noise, (K, WEEKS, PRODUCTS))
    week_part = jax.random.normal(key_week, (K, WEEKS, 1)) * 1.5
    product_part = jax.random.normal(key_prod, (K, 1, PRODUCTS)) * 2.0
    return jnp.clip(noise + week_part + product_part, -16.0, 16.0).astype(jnp.bfloat16)


def with_ends(result, own_key, smallest, high):
    longest = result.shape.index(max(result.shape))
    spots = []
    for shift in (0, 1):
        where = [jax.random.randint(jax.random.fold_in(own_key, axis), (), 0, length) for axis, length in enumerate(result.shape)]
        where[longest] = (where[longest] + shift) % result.shape[longest]
        spots.append(tuple(where))
    return result.at[spots[0]].set(smallest).at[spots[1]].set(high)


def setup_inputs(seed: int = 0) -> dict:
    arg_keys = jax.random.split(jax.random.key(seed), 5)
    return {
        "regressors": draw_regressors(jax.random.fold_in(arg_keys[4], 71), 0),
        "weights": with_ends(jax.random.randint(arg_keys[1], (WEEKS, PRODUCTS), 1, 5), jax.random.fold_in(arg_keys[1], 1), 1, 4).astype(jnp.int32),
        "first_week": draw_first_week(jax.random.fold_in(arg_keys[4], 71), 0),
        "last_week": draw_last_week(jax.random.fold_in(arg_keys[4], 71), 0),
    }


def reference(regressors, weights, first_week, last_week):
    week_ids = jnp.arange(WEEKS, dtype=jnp.int32)
    active = (week_ids[:, None] >= first_week[None, :]) & (week_ids[:, None] <= last_week[None, :])
    cell_weight = jnp.where(active, weights.astype(jnp.float32), jnp.float32(0.0))
    product_total = jnp.sum(cell_weight, axis=0)
    week_total = jnp.sum(cell_weight, axis=1)

    def column_sums(column):
        weighted = column.astype(jnp.float32) * cell_weight
        return jnp.sum(weighted, axis=0), jnp.sum(weighted, axis=1)

    product_sums, week_sums = lax.map(column_sums, regressors)
    week_effect = jnp.zeros((K, WEEKS), jnp.float32)
    product_effect = jnp.zeros((K, PRODUCTS), jnp.float32)
    for sweep in range(SWEEPS):
        product_effect = (product_sums - jnp.dot(week_effect, cell_weight, precision=lax.Precision.HIGHEST)) / product_total[None, :]
        week_effect = (week_sums - jnp.dot(product_effect, cell_weight.T, precision=lax.Precision.HIGHEST)) / week_total[None, :]

    def column_out(items):
        column, prod_part, week_part = items
        field = column.astype(jnp.float32) - prod_part[None, :] - week_part[:, None]
        return jnp.where(active, field, jnp.float32(0.0)).astype(jnp.bfloat16)

    demeaned = lax.map(column_out, (regressors, product_effect, week_effect))

    def block_step(carry, index):
        start = (index * P_DEV).astype(jnp.int32)
        values = lax.dynamic_slice_in_dim(regressors, start, P_DEV, 2).astype(jnp.float32)
        block_weight = lax.dynamic_slice_in_dim(cell_weight, start, P_DEV, 1)
        block_active = lax.dynamic_slice_in_dim(active, start, P_DEV, 1)
        block_effect = lax.dynamic_slice_in_dim(product_effect, start, P_DEV, 1)
        field = values - block_effect[:, None, :] - week_effect[:, :, None]
        field = jnp.where(block_active[None], field, jnp.float32(0.0))
        weighted = field * block_weight[None]
        return carry + jnp.einsum("kwp,lwp->kl", weighted, field, precision=lax.Precision.HIGHEST), None

    gram_sum, unused = lax.scan(block_step, jnp.zeros((K, K), jnp.float32), jnp.arange(PRODUCTS // P_DEV, dtype=jnp.int32))
    gram = gram_sum / jnp.sum(cell_weight)
    return demeaned, gram
```

```python
import functools

import jax
import jax.numpy as jnp
from jax import lax
from jax.experimental import pallas as pl
from jax.experimental.pallas import tpu as pltpu
from jax.sharding import PartitionSpec as P

MESH = pl.DeviceIdType.MESH
F32 = jnp.float32
BF16 = jnp.bfloat16
HI = lax.Precision.HIGHEST
NT = (((1,), (1,)), ((), ()))
NN = (((1,), (0,)), ((), ()))

K = 32
WK = 64
PD = 1536
NW = 8
NX = 4
NP = 32
WEEKS = NW * WK
LC = 384
HALF = PD // 2


def split3(v):
    hi = v.astype(BF16)
    r = v - hi.astype(F32)
    mid = r.astype(BF16)
    lo = (r - mid.astype(F32)).astype(BF16)
    return hi, mid, lo


def loop(lo, hi, body):
    def step(i, carry):
        body(i)
        return carry

    lax.fori_loop(lo, hi, step, 0)


def effects_kernel(
    x_hbm, weights, first, last,
    pe4_out, we4_out, gram_out,
    x, wfull, wb, pt_all, pt, ps_stage, ps_recv, pe1_chunks, pe1,
    b_pack, b_recv, b_all, m_stage, m_recv, mm,
    q_buf, u_buf, r_pack, r_week, r_prod, we_buf,
    x_sem, pt_s, pt_r, ps_s, ps_r, pe_s, pe_r, wx_s, wx_r, wc_s, wc_r,
    b_s, b_r, ba_s, ba_r, ms_s, ms_r, ma_s, ma_r, mx_s, mx_r, mc_s, mc_r,
    rw_s, rw_r, rp_s, rp_r,
):
    w = lax.axis_index("week")
    p = lax.axis_index("prod")
    xi = w // 2
    core = lax.rem(w, 2)
    sib = xi * 2 + (1 - core)

    def week_peer(d):
        return lax.rem(w + d, NW)

    def prod_peer(d):
        return lax.rem(p + d, NP)

    def x_peer(d):
        return lax.rem(xi + d, NX) * 2 + core

    def x_from(d):
        return lax.rem(xi + NX - d, NX) * 2 + core

    def to_week(src, dst, ssem, rsem, q):
        return pltpu.make_async_remote_copy(
            src_ref=src, dst_ref=dst, send_sem=ssem, recv_sem=rsem,
            device_id={"week": q}, device_id_type=MESH,
        )

    def to_prod(src, dst, ssem, rsem, q):
        return pltpu.make_async_remote_copy(
            src_ref=src, dst_ref=dst, send_sem=ssem, recv_sem=rsem,
            device_id={"prod": q}, device_id_type=MESH,
        )

    def x_copy(c):
        rows = pl.ds(c * 8, 8)
        return pltpu.make_async_copy(x_hbm.at[rows], x.at[rows], x_sem.at[c])

    for c in range(4):
        x_copy(c).start()

    barrier = pltpu.get_barrier_semaphore()

    def greet_week(d):
        pl.semaphore_signal(barrier, inc=1, device_id={"week": week_peer(d)}, device_id_type=MESH)

    def greet_prod(d):
        pl.semaphore_signal(barrier, inc=1, device_id={"prod": prod_peer(d)}, device_id_type=MESH)

    loop(1, NW, greet_week)
    loop(1, NP, greet_prod)

    wown = wfull.at[w]
    ids = w * WK + lax.broadcasted_iota(jnp.int32, (WK, PD), 0)
    live = (ids >= first[...]) & (ids <= last[...])
    cell = jnp.where(live, weights[...].astype(F32), 0.0)
    wown[...] = cell
    pt_all[w] = jnp.sum(cell, axis=0, keepdims=True)

    def ps_group(g):
        x_copy(g).wait()

        def one(j):
            k = g * 8 + j
            for c in range(PD // LC):
                lanes = slice(c * LC, (c + 1) * LC)
                weighted = x[k, :, lanes].astype(F32) * wfull[w, :, lanes]
                half, off = c // 2, (c % 2) * LC
                ps_stage[g * 2 + half, pl.ds(j, 1), off:off + LC] = jnp.sum(weighted, axis=0, keepdims=True)

        loop(0, 8, one)

    loop(0, 4, ps_group)

    pl.semaphore_wait(barrier, NW - 1 + NP - 1)

    def pt_copy(d):
        return to_week(pt_all.at[w], pt_all.at[w], pt_s.at[d], pt_r.at[d], week_peer(d))

    def pt_arrived(d):
        return to_week(pt_all.at[w], pt_all.at[lax.rem(w + NW - d, NW)], pt_s.at[d], pt_r.at[d], week_peer(d))

    def ps_copy(d):
        q = week_peer(d)
        return to_week(ps_stage.at[q], ps_recv.at[d], ps_s.at[d], ps_r.at[d], q)

    def send_ps(d):
        pt_copy(d).start()
        ps_copy(d).start()

    loop(1, NW, send_ps)

    def wx_copy(d):
        return to_week(wfull.at[w], wfull.at[w], wx_s.at[d], wx_r.at[d], x_peer(d))

    def wx_arrived(d):
        return to_week(wfull.at[w], wfull.at[x_from(d)], wx_s.at[d], wx_r.at[d], x_peer(d))

    def wc_copy(d):
        slot = x_from(d)
        return to_week(wfull.at[slot], wfull.at[slot], wc_s.at[d], wc_r.at[d], sib)

    def wc_arrived(d):
        slot = x_from(d)
        slot = slot + 1 - 2 * core
        return to_week(wfull.at[slot], wfull.at[slot], wc_s.at[d], wc_r.at[d], sib)

    for d in (1, 3, 2):
        wx_copy(d).start()
    wc_copy(0).start()

    def wait_ps(d):
        pt_arrived(d).wait_recv()
        ps_copy(d).wait_recv()

    loop(1, NW, wait_ps)
    pt[...] = jnp.sum(pt_all[...], axis=0)
    total = ps_stage[w]
    for d in range(1, NW):
        total = total + ps_recv[d]
    own_half = pl.ds(pl.multiple_of(lax.rem(w, 2) * HALF, HALF), HALF)
    pe1_chunks[w] = total / pt[:, own_half]

    def pe_copy(d):
        return to_week(pe1_chunks.at[w], pe1_chunks.at[w], pe_s.at[d], pe_r.at[d], week_peer(d))

    def pe_arrived(d):
        return to_week(pe1_chunks.at[w], pe1_chunks.at[lax.rem(w + NW - d, NW)], pe_s.at[d], pe_r.at[d], week_peer(d))

    loop(1, NW, lambda d: pe_copy(d).start())
    loop(1, NW, lambda d: pe_arrived(d).wait_recv())
    for r in range(NW):
        pe1[(r // 2) * 8:(r // 2) * 8 + 8, (r % 2) * HALF:(r % 2 + 1) * HALF] = pe1_chunks[r]

    lane = lax.broadcasted_iota(jnp.int32, (WK, 128), 1)

    def b_one(k, acc):
        part = jnp.zeros((WK, 128), F32)
        for c in range(PD // LC):
            lanes = slice(c * LC, (c + 1) * LC)
            f = (x[k, :, lanes].astype(F32) - pe1[pl.ds(k, 1), lanes]) * wfull[w, :, lanes]
            for t in range(LC // 128):
                part = part + f[:, t * 128:(t + 1) * 128]
        return acc + jnp.where(lane == k, jnp.sum(part, axis=1, keepdims=True), 0.0)

    wt_col = jnp.sum(wfull[w], axis=1, keepdims=True)
    bt = lax.fori_loop(0, K, b_one, jnp.where(lane == K, wt_col, 0.0))
    b_pack[...] = bt[:32] + pltpu.roll(bt[32:], 64, 1)

    def b_copy(d):
        return to_prod(b_pack, b_recv.at[d], b_s.at[d], b_r.at[d], prod_peer(d))

    loop(1, NP, lambda d: b_copy(d).start())

    for d in (1, 3, 2):
        wx_arrived(d).wait_recv()
        wc_copy(d).start()
    for d in (0, 1, 3, 2):
        wc_arrived(d).wait_recv()

    def to_bf16(i):
        wb[pl.ds(pl.multiple_of(i * WK, WK), WK), :] = wfull[i].astype(BF16)

    loop(0, NW, to_bf16)
    hi, mid, lo = split3(wfull[w] / pt[...])
    rows = jnp.concatenate([hi, mid, lo], axis=0)
    m3 = lax.dot_general(rows, wb[...], NT, preferred_element_type=F32)
    m_own = m3[:WK] + (m3[WK:2 * WK] + m3[2 * WK:])
    for q in range(NP):
        m_stage[q] = m_own[(q // 4) * 8:(q // 4) * 8 + 8, (q % 4) * 128:(q % 4 + 1) * 128]

    def ms_copy(d):
        q = prod_peer(d)
        return to_prod(m_stage.at[q], m_recv.at[d], ms_s.at[d], ms_r.at[d], q)

    loop(1, NP, lambda d: ms_copy(d).start())

    loop(1, NP, lambda d: b_copy(d).wait_recv())
    packed = lax.fori_loop(1, NP, lambda d, a: a + b_recv[d], b_pack[...])
    own_rows = pl.ds(pl.multiple_of(w * WK, WK), WK)
    b_all[own_rows, :] = jnp.concatenate([packed, pltpu.roll(packed, 64, 1)], axis=0)

    def ba_copy(d):
        return to_week(b_all.at[own_rows], b_all.at[own_rows], ba_s.at[d], ba_r.at[d], week_peer(d))

    def ba_arrived(d):
        other = pl.ds(pl.multiple_of(lax.rem(w + NW - d, NW) * WK, WK), WK)
        return to_week(b_all.at[own_rows], b_all.at[other], ba_s.at[d], ba_r.at[d], week_peer(d))

    loop(1, NW, lambda d: ba_copy(d).start())

    b_own = b_all[own_rows, :]
    wt_own = jnp.sum(jnp.where(lane == K, b_own, 0.0), axis=1, keepdims=True)
    we_buf[pl.ds(0, WK), :] = b_own / wt_own

    def r_pair(j):
        we1 = we_buf[pl.ds(0, WK), :]
        cols = [
            jnp.sum(jnp.where(lane == 2 * j + e, we1, 0.0), axis=1, keepdims=True)
            for e in range(2)
        ]
        at = pl.ds(pl.multiple_of(j * 16, 16), 16)
        for c in range(PD // 256):
            lanes = slice(c * 256, (c + 1) * 256)
            cellw = wfull[w, :, lanes]
            fs = []
            for e in range(2):
                k = 2 * j + e
                f = x[k, :, lanes].astype(F32) - pe1[pl.ds(k, 1), lanes] - cols[e]
                fs.append(jnp.where(cellw > 0.0, f, 0.0))
            for g in range(8):
                s = slice(g * 8, g * 8 + 8)
                pair = jnp.concatenate([fs[0][s], fs[1][s]], axis=0)
                wpair = jnp.concatenate([fs[0][s] * cellw[s], fs[1][s] * cellw[s]], axis=0)
                q_buf[g, at, lanes] = pair.astype(BF16)
                u_buf[g, at, lanes] = wpair.astype(BF16)

    loop(0, K // 2, r_pair)

    def r_dot(g, acc):
        return acc + lax.dot_general(u_buf[g], q_buf[g], NT, preferred_element_type=F32)

    big = lax.fori_loop(0, 8, r_dot, jnp.zeros((K * 8, K * 8), F32))
    ri = lax.broadcasted_iota(jnp.int32, (K * 8, K * 8), 0)
    ci = lax.broadcasted_iota(jnp.int32, (K * 8, K * 8), 1)
    big = jnp.where(lax.rem(ri, 8) == lax.rem(ci, 8), big, 0.0)
    ei = lax.broadcasted_iota(jnp.int32, (K, K * 8), 0)
    ej = lax.broadcasted_iota(jnp.int32, (K, K * 8), 1)
    fold = jnp.where(ei == ej // 8, 1.0, 0.0)
    fi = lax.broadcasted_iota(jnp.int32, (K * 8, 128), 0)
    fj = lax.broadcasted_iota(jnp.int32, (K * 8, 128), 1)
    fold_t = jnp.where(fi // 8 == fj, 1.0, 0.0)
    half_done = lax.dot_general(fold, big, NN, precision=HI, preferred_element_type=F32)
    r2 = lax.dot_general(half_done, fold_t, NN, precision=HI, preferred_element_type=F32)
    r_pack[0] = r2[0:8] + pltpu.roll(r2[8:16], 32, 1) + pltpu.roll(r2[16:24], 64, 1) + pltpu.roll(r2[24:32], 96, 1)

    def rw_copy(d):
        return to_week(r_pack.at[0], r_week.at[d], rw_s.at[d], rw_r.at[d], week_peer(d))

    loop(1, NW, lambda d: rw_copy(d).start())

    loop(1, NP, lambda d: ms_copy(d).wait_recv())
    tile = lax.fori_loop(1, NP, lambda d, a: a + m_recv[d], m_stage[p])

    def tile_of(wk, q):
        return mm.at[
            pl.ds(pl.multiple_of(wk * WK + (q // 4) * 8, 8), 8),
            pl.ds(pl.multiple_of(lax.rem(q, 4) * 128, 128), 128),
        ]

    tile_of(w, p)[...] = tile

    def ma_copy(d):
        return to_prod(tile_of(w, p), tile_of(w, p), ma_s.at[d], ma_r.at[d], prod_peer(d))

    def ma_arrived(d):
        return to_prod(tile_of(w, p), tile_of(w, lax.rem(p + NP - d, NP)), ma_s.at[d], ma_r.at[d], prod_peer(d))

    loop(1, NP, lambda d: ma_copy(d).start())

    loop(1, NW, lambda d: rw_copy(d).wait_recv())
    r_sum = r_pack[0]
    for d in range(1, NW):
        r_sum = r_sum + r_week[d]
    r_pack[1] = r_sum

    def rp_copy(d):
        return to_prod(r_pack.at[1], r_prod.at[d], rp_s.at[d], rp_r.at[d], prod_peer(d))

    loop(1, NP, lambda d: rp_copy(d).start())

    loop(1, NP, lambda d: ma_arrived(d).wait_recv())

    def rows_of(wk):
        return mm.at[pl.ds(pl.multiple_of(wk * WK, WK), WK)]

    def mx_copy(d):
        return to_week(rows_of(w), rows_of(w), mx_s.at[d], mx_r.at[d], x_peer(d))

    def mx_arrived(d):
        return to_week(rows_of(w), rows_of(x_from(d)), mx_s.at[d], mx_r.at[d], x_peer(d))

    def mc_copy(d):
        slot = x_from(d)
        return to_week(rows_of(slot), rows_of(slot), mc_s.at[d], mc_r.at[d], sib)

    def mc_arrived(d):
        slot = x_from(d) + 1 - 2 * core
        return to_week(rows_of(slot), rows_of(slot), mc_s.at[d], mc_r.at[d], sib)

    for d in (1, 3, 2):
        mx_copy(d).start()
    mc_copy(0).start()

    loop(1, NW, lambda d: ba_arrived(d).wait_recv())
    loop(1, NP, lambda d: rp_copy(d).wait_recv())
    r_total = lax.fori_loop(1, NP, lambda d, a: a + r_prod[d], r_pack[1])
    b = b_all[...]
    lane_all = lax.broadcasted_iota(jnp.int32, (WEEKS, 128), 1)
    wt = jnp.sum(jnp.where(lane_all == K, b, 0.0), axis=1, keepdims=True)
    b = jnp.where(lane_all < K, b, 0.0)
    we1 = b / wt
    weight_total = jnp.sum(wt, axis=0, keepdims=True)

    for d in (1, 3, 2):
        mx_arrived(d).wait_recv()
        mc_copy(d).start()
    for d in (0, 1, 3, 2):
        mc_arrived(d).wait_recv()

    def apply_m(v):
        return lax.dot_general(mm[...], v, NN, precision=HI, preferred_element_type=F32)

    n1 = apply_m(we1)
    we2 = (b + n1) / wt
    we3 = (b + apply_m(we2)) / wt
    n3 = apply_m(we3)
    we4 = (b + n3) / wt
    we_buf[...] = we4
    we4_out[...] = we_buf[own_rows, :]

    we3_t = we3.T[:K]
    hi, mid, lo = split3(we3_t)
    rows = jnp.concatenate([hi, mid, lo], axis=0)
    wp3 = lax.dot_general(rows, wb[...], NN, preferred_element_type=F32)
    wp = wp3[:K] + (wp3[K:2 * K] + wp3[2 * K:])
    pe4_out[...] = pe1[...] - wp / pt[...]

    gram = lax.dot_general((we3 - we4).T[:K], n3, NN, precision=HI, preferred_element_type=F32)
    gram = gram - lax.dot_general(we3_t, n1, NN, precision=HI, preferred_element_type=F32)
    r_rows = jnp.concatenate(
        [r_total] + [pltpu.roll(r_total, 128 - 32 * a, 1) for a in range(1, 4)], axis=0
    )
    gram_out[...] = ((r_rows + gram) / weight_total)[:, :K]

    def drain_week(d):
        pt_copy(d).wait_send()
        ps_copy(d).wait_send()
        pe_copy(d).wait_send()
        ba_copy(d).wait_send()
        rw_copy(d).wait_send()

    loop(1, NW, drain_week)

    def drain_prod(d):
        b_copy(d).wait_send()
        ms_copy(d).wait_send()
        ma_copy(d).wait_send()
        rp_copy(d).wait_send()

    loop(1, NP, drain_prod)
    for d in range(NX):
        if d:
            wx_copy(d).wait_send()
            mx_copy(d).wait_send()
        wc_copy(d).wait_send()
        mc_copy(d).wait_send()


def effects(x, weights, first, last):
    vmem = pl.BlockSpec(memory_space=pltpu.VMEM)
    dma = pltpu.SemaphoreType.DMA
    scratch = [
        pltpu.VMEM((K, WK, PD), BF16),
        pltpu.VMEM((NW, WK, PD), F32),
        pltpu.VMEM((WEEKS, PD), BF16),
        pltpu.VMEM((NW, 1, PD), F32),
        pltpu.VMEM((1, PD), F32),
        pltpu.VMEM((NW, 8, HALF), F32),
        pltpu.VMEM((NW, 8, HALF), F32),
        pltpu.VMEM((NW, 8, HALF), F32),
        pltpu.VMEM((K, PD), F32),
        pltpu.VMEM((32, 128), F32),
        pltpu.VMEM((NP, 32, 128), F32),
        pltpu.VMEM((WEEKS, 128), F32),
        pltpu.VMEM((NP, 8, 128), F32),
        pltpu.VMEM((NP, 8, 128), F32),
        pltpu.VMEM((WEEKS, WEEKS), F32),
        pltpu.VMEM((8, K * 8, PD), BF16),
        pltpu.VMEM((8, K * 8, PD), BF16),
        pltpu.VMEM((2, 8, 128), F32),
        pltpu.VMEM((NW, 8, 128), F32),
        pltpu.VMEM((NP, 8, 128), F32),
        pltpu.VMEM((WEEKS, 128), F32),
        dma((4,)),
    ]
    for n in (NW, NW, NW, NX, NX, NP, NW, NP, NP, NX, NX, NW, NP):
        scratch += [dma((n,)), dma((n,))]
    return pl.pallas_call(
        effects_kernel,
        out_shape=(
            jax.ShapeDtypeStruct((K, PD), F32),
            jax.ShapeDtypeStruct((WK, 128), F32),
            jax.ShapeDtypeStruct((K, K), F32),
        ),
        in_specs=[pl.BlockSpec(memory_space=pl.ANY), vmem, vmem, vmem],
        out_specs=(vmem, vmem, vmem),
        scratch_shapes=scratch,
        compiler_params=pltpu.CompilerParams(
            collective_id=0, has_side_effects=True, vmem_limit_bytes=48 * 2**20
        ),
        name="effects",
    )(x, weights, first, last)


def per_device(regressors, weights, first_week, last_week):
    first = first_week.reshape(1, PD)
    last = last_week.reshape(1, PD)
    pe4, we4, gram = effects(regressors, weights, first, last)
    ids = lax.axis_index("week") * WK + lax.broadcasted_iota(jnp.int32, (WK, PD), 0)
    live = (ids >= first) & (ids <= last)
    field = regressors.astype(F32) - pe4[:, None, :] - we4[:, :K].T[:, :, None]
    return jnp.where(live[None], field, 0.0).astype(BF16), gram


def solution(mesh):
    return jax.shard_map(
        per_device,
        mesh=mesh,
        in_specs=(P(None, "week", "prod"), P("week", "prod"), P("prod"), P("prod")),
        out_specs=(P(None, "week", "prod"), P()),
        check_vma=False,
    )
```

```python
import functools

import jax
import jax.numpy as jnp
from jax import lax
from jax.experimental import pallas as pl
from jax.experimental.pallas import tpu as pltpu
from jax.sharding import PartitionSpec as P

MESH = pl.DeviceIdType.MESH
F32 = jnp.float32
BF16 = jnp.bfloat16
HI = lax.Precision.HIGHEST
NT = (((1,), (1,)), ((), ()))
NN = (((1,), (0,)), ((), ()))

K = 32
WK = 64
PD = 1536
NW = 8
NX = 4
NP = 32
WEEKS = NW * WK
LC = 384
HALF = PD // 2
W_PARTS = (0, 16, 40, 64)


def split3(v):
    hi = v.astype(BF16)
    r = v - hi.astype(F32)
    mid = r.astype(BF16)
    lo = (r - mid.astype(F32)).astype(BF16)
    return hi, mid, lo


def loop(lo, hi, body):
    def step(i, carry):
        body(i)
        return carry

    lax.fori_loop(lo, hi, step, 0)


class Transfer:
    def __init__(self, ds, send, arrival=None):
        self.ds, self.send, self.arrival = ds, send, arrival or send
        self.sent, self.got = [], []

    def each(self, ds, act):
        if isinstance(ds, range) and len(ds) > 3:
            loop(ds.start, ds.stop, act)
        else:
            for d in ds:
                act(d)

    def start(self, ds=None):
        ds = self.ds if ds is None else ds
        self.each(ds, lambda d: self.send(d).start())
        self.sent += list(ds)

    def wait(self, ds=None):
        ds = self.ds if ds is None else ds
        self.each(ds, lambda d: self.arrival(d).wait_recv())
        self.got += list(ds)

    def drain(self):
        self.each(self.ds if len(self.sent) == len(self.ds) else self.sent, lambda d: self.send(d).wait_send())


def effects_kernel(
    x_hbm, weights_hbm, first_hbm, last_hbm,
    pe4_out, we4_out, gram_out,
    x, weights, first, last, wfull, wb, pt_own, pt_sib, pt_all, pt, wt_part, ps_stage, ps_sib, ps_recv, pe1_chunks, pe1,
    b_pack, b_recv, b_all, m_stage, m_recv, mm, m_hi, m_mid, m_lo,
    q_buf, u_buf, r_pack, r_week, r_prod, we_buf,
    x_sem, pt_s, pt_r, ps_s, ps_r, wt_s, wt_r, pe_s, pe_r, pf_s, pf_r, wx_s, wx_r, wc_s, wc_r, wy_s, wy_r, wd_s, wd_r,
    b_s, b_r, ba_s, ba_r, ms_s, ms_r, ma_s, ma_r, mx_s, mx_r, mc_s, mc_r,
    rw_s, rw_r, rp_s, rp_r,
):
    w = lax.axis_index("week")
    p = lax.axis_index("prod")
    xi = w // 2
    core = lax.rem(w, 2)
    sib = xi * 2 + (1 - core)

    def week_peer(d):
        return lax.rem(w + d, NW)

    def prod_peer(d):
        return lax.rem(p + d, NP)

    def x_peer(d):
        return lax.rem(xi + d, NX) * 2 + core

    def x_from(d):
        return lax.rem(xi + NX - d, NX) * 2 + core

    def to_week(src, dst, ssem, rsem, q):
        return pltpu.make_async_remote_copy(
            src_ref=src, dst_ref=dst, send_sem=ssem, recv_sem=rsem,
            device_id={"week": q}, device_id_type=MESH,
        )

    def to_prod(src, dst, ssem, rsem, q):
        return pltpu.make_async_remote_copy(
            src_ref=src, dst_ref=dst, send_sem=ssem, recv_sem=rsem,
            device_id={"prod": q}, device_id_type=MESH,
        )

    def x_copy(c):
        rows = pl.ds(c * 8, 8)
        return pltpu.make_async_copy(x_hbm.at[rows], x.at[rows], x_sem.at[c])

    weights_copy = pltpu.make_async_copy(weights_hbm, weights, x_sem.at[4])
    weights_copy.start()
    first_copy = pltpu.make_async_copy(first_hbm, first, x_sem.at[5])
    first_copy.start()
    last_copy = pltpu.make_async_copy(last_hbm, last, x_sem.at[6])
    last_copy.start()
    for c in range(4):
        x_copy(c).start()

    barrier = pltpu.get_barrier_semaphore()

    def greet_week(d):
        pl.semaphore_signal(barrier, inc=1, device_id={"week": week_peer(d)}, device_id_type=MESH)

    def greet_prod(d):
        pl.semaphore_signal(barrier, inc=1, device_id={"prod": prod_peer(d)}, device_id_type=MESH)

    loop(1, NW, greet_week)
    loop(1, NP, greet_prod)

    weights_copy.wait()
    first_copy.wait()
    last_copy.wait()
    ids = w * WK + lax.broadcasted_iota(jnp.int32, (WK, PD), 0)
    live = (ids >= first[...].reshape(1, PD)) & (ids <= last[...].reshape(1, PD))
    cell = jnp.where(live, weights[...].astype(F32), 0.0)
    wfull[w] = cell
    wb[pl.ds(pl.multiple_of(w * WK, WK), WK), :] = cell.astype(BF16)
    pt_own[...] = jnp.sum(cell, axis=0, keepdims=True)
    lane = lax.broadcasted_iota(jnp.int32, (WK, 128), 1)
    row = lax.broadcasted_iota(jnp.int32, (WK, 128), 0)
    wt_col = jnp.sum(cell, axis=1, keepdims=True)
    wt_part[p] = jnp.sum(jnp.where(lane == row, wt_col, 0.0), axis=0, keepdims=True)

    def sums_group(g, acc):
        x_copy(g).wait()

        def one(j, acc):
            k = g * 8 + j
            part = jnp.zeros((WK, 128), F32)
            for c in range(PD // LC):
                lanes = slice(c * LC, (c + 1) * LC)
                weighted = x[k, :, lanes].astype(F32) * wfull[w, :, lanes]
                half, off = c // 2, (c % 2) * LC
                ps_stage[half, g, pl.ds(j, 1), off:off + LC] = jnp.sum(weighted, axis=0, keepdims=True)
                for t in range(LC // 128):
                    part = part + weighted[:, t * 128:(t + 1) * 128]
            return acc + jnp.where(lane == k, jnp.sum(part, axis=1, keepdims=True), 0.0)

        return lax.fori_loop(0, 8, one, acc, unroll=2)

    ws = lax.fori_loop(0, 4, sums_group, jnp.zeros((WK, 128), F32))

    pl.semaphore_wait(barrier, NW - 1 + NP - 1)

    def pt_copy(d):
        if d == 0:
            return to_week(pt_own, pt_sib, pt_s.at[0], pt_r.at[0], sib)
        return to_week(pt_all.at[xi], pt_all.at[xi], pt_s.at[d], pt_r.at[d], x_peer(d))

    def pt_arrived(d):
        if d == 0:
            return pt_copy(0)
        return to_week(pt_all.at[xi], pt_all.at[lax.rem(xi + NX - d, NX)], pt_s.at[d], pt_r.at[d], x_peer(d))

    def ps_copy(d):
        if d == 0:
            return to_week(ps_stage.at[1 - core], ps_sib, ps_s.at[0], ps_r.at[0], sib)
        q = x_peer(d)
        return to_week(ps_stage.at[core, lax.rem(xi + d, NX)], ps_recv.at[d], ps_s.at[d], ps_r.at[d], q)

    pt_move = Transfer((0, 2, 1, 3), pt_copy, pt_arrived)
    ps_move = Transfer((0, 2, 1, 3), ps_copy)
    pt_move.start((0,))
    ps_move.start((0,))

    def wt_copy(d):
        return to_prod(wt_part.at[p], wt_part.at[p], wt_s.at[d], wt_r.at[d], prod_peer(d))

    def wt_arrived(d):
        return to_prod(wt_part.at[p], wt_part.at[lax.rem(p + NP - d, NP)], wt_s.at[d], wt_r.at[d], prod_peer(d))

    def first_half(chip, other):
        return jnp.where(chip < other, 0, 1)

    def half_of(slot, h):
        return wfull.at[slot, :, pl.ds(pl.multiple_of(h * HALF, HALF), HALF)]

    def chip_to(d):
        return lax.rem(xi + d, NX)

    def chip_from(d):
        return lax.rem(xi + NX - d, NX)

    def part_of(slot, h, e):
        lo, hi = W_PARTS[e], W_PARTS[e + 1]
        return wfull.at[slot, pl.ds(lo, hi - lo), pl.ds(pl.multiple_of(h * HALF, HALF), HALF)]

    def wx_copy(i):
        d, e = i % NX, i // NX
        h = first_half(chip_to(d), xi)
        return to_week(part_of(w, h, e), part_of(w, h, e), wx_s.at[i], wx_r.at[i], x_peer(d))

    def wx_arrived(i):
        d, e = i % NX, i // NX
        h = first_half(xi, chip_from(d))
        return to_week(part_of(w, h, e), part_of(x_from(d), h, e), wx_s.at[i], wx_r.at[i], x_peer(d))

    def wy_copy(d):
        h = 1 - first_half(chip_to(d), xi)
        return to_week(half_of(w, h), half_of(w, h), wy_s.at[d], wy_r.at[d], x_peer(d))

    def wy_arrived(d):
        h = 1 - first_half(xi, chip_from(d))
        return to_week(half_of(w, h), half_of(x_from(d), h), wy_s.at[d], wy_r.at[d], x_peer(d))

    def other_core(slot):
        return slot + 1 - 2 * core

    def wc_copy(i):
        d, e = i % NX, i // NX
        if d == 0:
            return to_week(wfull.at[w], wfull.at[w], wc_s.at[i], wc_r.at[i], sib)
        here = part_of(x_from(d), first_half(xi, chip_from(d)), e)
        return to_week(here, here, wc_s.at[i], wc_r.at[i], sib)

    def wc_arrived(i):
        d, e = i % NX, i // NX
        if d == 0:
            return to_week(wfull.at[w], wfull.at[sib], wc_s.at[i], wc_r.at[i], sib)
        here = part_of(other_core(x_from(d)), first_half(xi, chip_from(d)), e)
        return to_week(here, here, wc_s.at[i], wc_r.at[i], sib)

    def wd_copy(d):
        here = half_of(x_from(d), 1 - first_half(xi, chip_from(d)))
        return to_week(here, here, wd_s.at[d], wd_r.at[d], sib)

    def wd_arrived(d):
        here = half_of(other_core(x_from(d)), 1 - first_half(xi, chip_from(d)))
        return to_week(here, here, wd_s.at[d], wd_r.at[d], sib)

    wt_move = Transfer(range(1, NP), wt_copy, wt_arrived)
    wt_move.start()
    parts = range(len(W_PARTS) - 1)
    wx_move = Transfer([d + NX * e for e in parts for d in (2, 1, 3)], wx_copy, wx_arrived)
    wc_move = Transfer([0] + [d + NX * e for e in parts for d in (1, 3, 2)], wc_copy, wc_arrived)
    wy_move = Transfer((2, 1, 3), wy_copy, wy_arrived)
    wd_move = Transfer((1, 3, 2), wd_copy, wd_arrived)

    def send_part(e):
        wx_move.start([d + NX * e for d in (2, 1, 3)])

    send_part(0)
    pt_move.wait((0,))
    pt_all[xi] = pt_own[...] + pt_sib[...]
    ps_move.wait((0,))
    for a in range(NX):
        ps_stage[core, a] = ps_stage[core, a] + ps_sib[a]
    pt_move.start((2, 1, 3))
    ps_move.start((2, 1, 3))
    wc_move.start((0,))
    send_part(1)
    pt_move.wait((2, 1, 3))
    ps_move.wait((2, 1, 3))
    pt[...] = jnp.sum(pt_all[...], axis=0)
    total = ps_stage[core, xi]
    for d in range(1, NX):
        total = total + ps_recv[d]
    own_half = pl.ds(pl.multiple_of(core * HALF, HALF), HALF)
    pe1_chunks[w] = total / pt[:, own_half]

    def pe_copy(d):
        return to_week(pe1_chunks.at[w], pe1_chunks.at[w], pe_s.at[d], pe_r.at[d], x_peer(d))

    def pe_arrived(d):
        return to_week(pe1_chunks.at[w], pe1_chunks.at[x_from(d)], pe_s.at[d], pe_r.at[d], x_peer(d))

    def pf_copy(d):
        slot = x_from(d)
        return to_week(pe1_chunks.at[slot], pe1_chunks.at[slot], pf_s.at[d], pf_r.at[d], sib)

    def pf_arrived(d):
        slot = other_core(x_from(d))
        return to_week(pe1_chunks.at[slot], pe1_chunks.at[slot], pf_s.at[d], pf_r.at[d], sib)

    pe_move = Transfer((2, 1, 3), pe_copy, pe_arrived)
    pf_move = Transfer((0, 1, 3, 2), pf_copy, pf_arrived)
    pe_move.start()
    pf_move.start((0,))
    for e in parts[2:]:
        send_part(e)

    def wb_half(slot, h):
        return wb.at[
            pl.ds(pl.multiple_of(slot * WK, WK), WK),
            pl.ds(pl.multiple_of(h * HALF, HALF), HALF),
        ]

    for e in parts[:2]:
        for d in (1, 3, 2):
            wx_move.wait((d + NX * e,))
            wc_move.start((d + NX * e,))

    for d in (1, 3, 2):
        pe_move.wait((d,))
        pf_move.start((d,))
    pf_move.wait()
    for r in range(NW):
        pe1[(r // 2) * 8:(r // 2) * 8 + 8, (r % 2) * HALF:(r % 2 + 1) * HALF] = pe1_chunks[r]
    hi, mid, lo = split3(pe1[...])
    pe_rows = jnp.concatenate([hi, mid, lo, jnp.zeros((K, PD), BF16)], axis=0)
    own_wb = wb[pl.ds(pl.multiple_of(w * WK, WK), WK), :]
    taken = lax.dot_general(own_wb, pe_rows, NT, preferred_element_type=F32)
    taken = taken + (pltpu.roll(taken, 128 - K, 1) + pltpu.roll(taken, 128 - 2 * K, 1))
    bt = jnp.where(lane < K, ws - taken, 0.0)
    b_pack[...] = sum(
        [pltpu.roll(bt[16 * a:16 * a + 16], 32 * a, 1) for a in range(1, 4)], bt[:16]
    )

    def b_copy(d):
        return to_prod(b_pack, b_recv.at[d], b_s.at[d], b_r.at[d], prod_peer(d))

    b_move = Transfer(range(1, NP), b_copy)
    b_move.start()

    for e in parts[2:]:
        for d in (1, 3, 2):
            wx_move.wait((d + NX * e,))
            wc_move.start((d + NX * e,))
    hi, mid, lo = split3(wfull[w] / pt[...])
    wc_move.wait()

    for h in (0, 1):
        wb_half(sib, h)[...] = half_of(sib, h)[...].astype(BF16)

    def to_bf16(i):
        d = 1 + i // 2
        slot = chip_from(d) * 2 + lax.rem(i, 2)
        h = first_half(xi, chip_from(d))
        wb_half(slot, h)[...] = half_of(slot, h)[...].astype(BF16)
        wb_half(slot, 1 - h)[...] = jnp.zeros((WK, HALF), BF16)

    loop(0, NW - 2, to_bf16)
    rows = jnp.concatenate([hi, mid, lo], axis=0)
    m3 = lax.dot_general(rows, wb[...], NT, preferred_element_type=F32)
    m_own = m3[:WK] + (m3[WK:2 * WK] + m3[2 * WK:])
    for q in range(NP):
        m_stage[q] = m_own[(q // 4) * 8:(q // 4) * 8 + 8, (q % 4) * 128:(q % 4 + 1) * 128]

    def ms_copy(d):
        q = prod_peer(d)
        return to_prod(m_stage.at[q], m_recv.at[d], ms_s.at[d], ms_r.at[d], q)

    ms_move = Transfer(range(1, NP), ms_copy)
    ms_move.start()
    wy_move.start()

    b_move.wait()
    wt_move.wait()
    wt_row = lax.fori_loop(0, NP, lambda d, a: a + wt_part[d], jnp.zeros((1, 128), F32))
    wt_own = jnp.sum(jnp.where(lane == row, wt_row, 0.0), axis=1, keepdims=True)
    packed = lax.fori_loop(1, NP, lambda d, a: a + b_recv[d], b_pack[...])
    b_own = jnp.concatenate(
        [packed] + [pltpu.roll(packed, 128 - 32 * a, 1) for a in range(1, 4)], axis=0
    )
    b_own = jnp.where(lane < K, b_own, jnp.where(lane == K, wt_own, 0.0))
    b_all[w] = b_own[:32] + pltpu.roll(b_own[32:], 64, 1)
    own_rows = pl.ds(pl.multiple_of(w * WK, WK), WK)

    def ba_copy(d):
        return to_week(b_all.at[w], b_all.at[w], ba_s.at[d], ba_r.at[d], week_peer(d))

    def ba_arrived(d):
        return to_week(b_all.at[w], b_all.at[lax.rem(w + NW - d, NW)], ba_s.at[d], ba_r.at[d], week_peer(d))

    ba_move = Transfer(range(1, NW), ba_copy, ba_arrived)
    ba_move.start()

    we_buf[pl.ds(0, WK), :] = b_own / wt_own

    def r_pair(j):
        we1 = we_buf[pl.ds(0, WK), :]
        cols = [
            jnp.sum(jnp.where(lane == 2 * j + e, we1, 0.0), axis=1, keepdims=True)
            for e in range(2)
        ]
        at = pl.ds(pl.multiple_of(j * 16, 16), 16)
        for c in range(PD // 256):
            lanes = slice(c * 256, (c + 1) * 256)
            cellw = wfull[w, :, lanes]
            fs = []
            for e in range(2):
                k = 2 * j + e
                f = x[k, :, lanes].astype(F32) - pe1[pl.ds(k, 1), lanes] - cols[e]
                fs.append(jnp.where(cellw > 0.0, f, 0.0))
            for g in range(8):
                s = slice(g * 8, g * 8 + 8)
                pair = jnp.concatenate([fs[0][s], fs[1][s]], axis=0)
                wpair = jnp.concatenate([fs[0][s] * cellw[s], fs[1][s] * cellw[s]], axis=0)
                q_buf[g, at, lanes] = pair.astype(BF16)
                u_buf[g, at, lanes] = wpair.astype(BF16)

    loop(0, K // 2, r_pair)

    ms_move.wait()
    tile = lax.fori_loop(1, NP, lambda d, a: a + m_recv[d], m_stage[p])

    def tile_of(wk, q):
        return mm.at[
            pl.ds(pl.multiple_of(wk * WK + (q // 4) * 8, 8), 8),
            pl.ds(pl.multiple_of(lax.rem(q, 4) * 128, 128), 128),
        ]

    tile_of(w, p)[...] = tile

    def ma_copy(d):
        return to_prod(tile_of(w, p), tile_of(w, p), ma_s.at[d], ma_r.at[d], prod_peer(d))

    def ma_arrived(d):
        return to_prod(tile_of(w, p), tile_of(w, lax.rem(p + NP - d, NP)), ma_s.at[d], ma_r.at[d], prod_peer(d))

    ma_move = Transfer(range(1, NP), ma_copy, ma_arrived)
    ma_move.start()

    def r_dot(g, acc):
        return acc + lax.dot_general(u_buf[g], q_buf[g], NT, preferred_element_type=F32)

    big = lax.fori_loop(0, 8, r_dot, jnp.zeros((K * 8, K * 8), F32))
    ri = lax.broadcasted_iota(jnp.int32, (K * 8, K * 8), 0)
    ci = lax.broadcasted_iota(jnp.int32, (K * 8, K * 8), 1)
    big = jnp.where(lax.rem(ri, 8) == lax.rem(ci, 8), big, 0.0)
    ei = lax.broadcasted_iota(jnp.int32, (K, K * 8), 0)
    ej = lax.broadcasted_iota(jnp.int32, (K, K * 8), 1)
    fold = jnp.where(ei == ej // 8, 1.0, 0.0)
    fi = lax.broadcasted_iota(jnp.int32, (K * 8, 128), 0)
    fj = lax.broadcasted_iota(jnp.int32, (K * 8, 128), 1)
    fold_t = jnp.where(fi // 8 == fj, 1.0, 0.0)
    half_done = lax.dot_general(fold, big, NN, precision=HI, preferred_element_type=F32)
    r2 = lax.dot_general(half_done, fold_t, NN, precision=HI, preferred_element_type=F32)
    r_pack[0] = r2[0:8] + pltpu.roll(r2[8:16], 32, 1) + pltpu.roll(r2[16:24], 64, 1) + pltpu.roll(r2[24:32], 96, 1)

    def rw_copy(d):
        return to_week(r_pack.at[0], r_week.at[d], rw_s.at[d], rw_r.at[d], week_peer(d))

    rw_move = Transfer(range(1, NW), rw_copy)
    rw_move.start()

    ma_move.wait()

    def rows_of(wk):
        return mm.at[pl.ds(pl.multiple_of(wk * WK, WK), WK)]

    def mx_copy(d):
        return to_week(rows_of(w), rows_of(w), mx_s.at[d], mx_r.at[d], x_peer(d))

    def mx_arrived(d):
        return to_week(rows_of(w), rows_of(x_from(d)), mx_s.at[d], mx_r.at[d], x_peer(d))

    def mc_copy(d):
        slot = x_from(d)
        return to_week(rows_of(slot), rows_of(slot), mc_s.at[d], mc_r.at[d], sib)

    def mc_arrived(d):
        slot = x_from(d) + 1 - 2 * core
        return to_week(rows_of(slot), rows_of(slot), mc_s.at[d], mc_r.at[d], sib)

    mx_move = Transfer((1, 3, 2), mx_copy, mx_arrived)
    mc_move = Transfer((0, 1, 3, 2), mc_copy, mc_arrived)
    mx_move.start()
    mc_move.start((0,))

    rw_move.wait()
    r_sum = r_pack[0]
    for d in range(1, NW):
        r_sum = r_sum + r_week[d]
    r_pack[1] = r_sum

    def rp_copy(d):
        return to_prod(r_pack.at[1], r_prod.at[d], rp_s.at[d], rp_r.at[d], prod_peer(d))

    rp_move = Transfer(range(1, NP), rp_copy)
    rp_move.start()
    for d in (1, 3, 2):
        mx_move.wait((d,))
        mc_move.start((d,))
    for d in (1, 3, 2):
        wy_move.wait((d,))
        wd_move.start((d,))
    wd_move.wait()

    def rest_to_bf16(i):
        d = 1 + i // 2
        slot = chip_from(d) * 2 + lax.rem(i, 2)
        h = 1 - first_half(xi, chip_from(d))
        wb_half(slot, h)[...] = half_of(slot, h)[...].astype(BF16)

    loop(0, NW - 2, rest_to_bf16)

    ba_move.wait()
    lane_all = lax.broadcasted_iota(jnp.int32, (WEEKS, 128), 1)
    pieces = []
    for i in range(NW):
        piece = b_all[i]
        pieces += [piece, pltpu.roll(piece, 64, 1)]
    b = jnp.concatenate(pieces, axis=0)
    wt = jnp.sum(jnp.where(lane_all == K, b, 0.0), axis=1, keepdims=True)
    b = jnp.where(lane_all < K, b, 0.0)
    we1 = b / wt
    weight_total = jnp.sum(wt, axis=0, keepdims=True)

    mc_move.wait()

    def put_m(rows, cols, v):
        hi, mid, lo = split3(v)
        m_hi[rows, cols] = hi
        m_mid[rows, cols] = mid
        m_lo[rows, cols] = lo

    blocks = [slice(a * 128, a * 128 + 128) for a in range(NX)]
    for a in range(NX):
        put_m(blocks[a], blocks[a], mm[blocks[a], blocks[a]])
        for c in range(a + 1, NX):
            both = mm[blocks[a], blocks[c]] + mm[blocks[c], blocks[a]].T
            put_m(blocks[a], blocks[c], both)
            put_m(blocks[c], blocks[a], both.T)

    def apply_m(v):
        hi, mid, lo = [part.astype(F32) for part in split3(v)]
        parts = (hi + pltpu.roll(mid, K, 1) + pltpu.roll(lo, 2 * K, 1)).astype(BF16)
        acc = jnp.dot(m_hi[...], parts, preferred_element_type=F32)
        acc = acc + jnp.where(lane_all < 2 * K, jnp.dot(m_mid[...], parts, preferred_element_type=F32), 0.0)
        acc = acc + jnp.where(lane_all < K, jnp.dot(m_lo[...], parts, preferred_element_type=F32), 0.0)
        acc = acc + (pltpu.roll(acc, 128 - K, 1) + pltpu.roll(acc, 128 - 2 * K, 1))
        return jnp.where(lane_all < K, acc, 0.0)

    n1 = apply_m(we1)
    we2 = (b + n1) / wt
    we3 = (b + apply_m(we2)) / wt
    n3 = apply_m(we3)
    we4 = (b + n3) / wt
    we_buf[...] = we4
    we4_out[...] = we_buf[own_rows, :]

    we3_t = we3.T[:K]
    hi, mid, lo = split3(we3_t)
    rows = jnp.concatenate([hi, mid, lo], axis=0)
    wp3 = lax.dot_general(rows, wb[...], NN, preferred_element_type=F32)
    wp = wp3[:K] + (wp3[K:2 * K] + wp3[2 * K:])
    pe4_out[...] = pe1[...] - wp / pt[...]

    rp_move.wait()
    r_total = lax.fori_loop(1, NP, lambda d, a: a + r_prod[d], r_pack[1])
    gram = lax.dot_general((we3 - we4).T[:K], n3, NN, precision=HI, preferred_element_type=F32)
    gram = gram - lax.dot_general(we3_t, n1, NN, precision=HI, preferred_element_type=F32)
    r_rows = jnp.concatenate(
        [r_total] + [pltpu.roll(r_total, 128 - 32 * a, 1) for a in range(1, 4)], axis=0
    )
    gram_out[...] = ((r_rows + gram) / weight_total)[:, :K]

    for move in (
        pt_move, ps_move, wt_move, wx_move, wc_move, wy_move, wd_move, pe_move, pf_move, b_move, ba_move,
        ms_move, ma_move, mx_move, mc_move, rw_move, rp_move,
    ):
        move.drain()


def effects(x, weights, first, last):
    vmem = pl.BlockSpec(memory_space=pltpu.VMEM)
    dma = pltpu.SemaphoreType.DMA
    scratch = [
        pltpu.VMEM((K, WK, PD), BF16),
        pltpu.VMEM((WK, PD), jnp.int32),
        pltpu.VMEM((PD,), jnp.int32),
        pltpu.VMEM((PD,), jnp.int32),
        pltpu.VMEM((NW, WK, PD), F32),
        pltpu.VMEM((WEEKS, PD), BF16),
        pltpu.VMEM((1, PD), F32),
        pltpu.VMEM((1, PD), F32),
        pltpu.VMEM((NX, 1, PD), F32),
        pltpu.VMEM((1, PD), F32),
        pltpu.VMEM((NP, 1, 128), F32),
        pltpu.VMEM((2, NX, 8, HALF), F32),
        pltpu.VMEM((NX, 8, HALF), F32),
        pltpu.VMEM((NX, 8, HALF), F32),
        pltpu.VMEM((NW, 8, HALF), F32),
        pltpu.VMEM((K, PD), F32),
        pltpu.VMEM((16, 128), F32),
        pltpu.VMEM((NP, 16, 128), F32),
        pltpu.VMEM((NW, 32, 128), F32),
        pltpu.VMEM((NP, 8, 128), F32),
        pltpu.VMEM((NP, 8, 128), F32),
        pltpu.VMEM((WEEKS, WEEKS), F32),
        pltpu.VMEM((WEEKS, WEEKS), BF16),
        pltpu.VMEM((WEEKS, WEEKS), BF16),
        pltpu.VMEM((WEEKS, WEEKS), BF16),
        pltpu.VMEM((8, K * 8, PD), BF16),
        pltpu.VMEM((8, K * 8, PD), BF16),
        pltpu.VMEM((2, 8, 128), F32),
        pltpu.VMEM((NW, 8, 128), F32),
        pltpu.VMEM((NP, 8, 128), F32),
        pltpu.VMEM((WEEKS, 128), F32),
        dma((7,)),
    ]
    for n in (NX, NX, NP, NX, NX, len(W_PARTS) * NX, len(W_PARTS) * NX, NX, NX, NP, NW, NP, NP, NX, NX, NW, NP):
        scratch += [dma((n,)), dma((n,))]
    return pl.pallas_call(
        effects_kernel,
        out_shape=(
            jax.ShapeDtypeStruct((K, PD), F32),
            jax.ShapeDtypeStruct((WK, 128), F32),
            jax.ShapeDtypeStruct((K, K), F32),
        ),
        in_specs=[pl.BlockSpec(memory_space=pl.ANY)] * 4,
        out_specs=(vmem, vmem, vmem),
        scratch_shapes=scratch,
        compiler_params=pltpu.CompilerParams(
            collective_id=0, has_side_effects=True, vmem_limit_bytes=48 * 2**20
        ),
        name="effects",
    )(x, weights, first, last)


KB = 4


def output_kernel(x, first, last, pe4, we4, gram, out, gram_out):
    w = lax.axis_index("week")
    step = pl.program_id(0)
    gram_out[...] = gram[...]
    lane = lax.broadcasted_iota(jnp.int32, (WK, 128), 1)
    ids = w * WK + lax.broadcasted_iota(jnp.int32, (WK, LC), 0)
    cols = [
        jnp.sum(jnp.where(lane == step * KB + e, we4[...], 0.0), axis=1, keepdims=True)
        for e in range(KB)
    ]
    first_row = first[...].reshape(1, PD)
    last_row = last[...].reshape(1, PD)
    for c in range(PD // LC):
        lanes = slice(c * LC, (c + 1) * LC)
        live = (ids >= first_row[:, lanes]) & (ids <= last_row[:, lanes])
        for e in range(KB):
            field = x[e, :, lanes].astype(F32) - pe4[pl.ds(step * KB + e, 1), lanes] - cols[e]
            out[e, :, lanes] = jnp.where(live, field, 0.0).astype(BF16)


def output(x, first, last, pe4, we4, gram):
    vmem = pl.BlockSpec(memory_space=pltpu.VMEM)
    block = pl.BlockSpec((KB, WK, PD), lambda i: (i, 0, 0))
    return pl.pallas_call(
        output_kernel,
        grid=(K // KB,),
        out_shape=(
            jax.ShapeDtypeStruct((K, WK, PD), BF16),
            jax.ShapeDtypeStruct((K, K), F32),
        ),
        in_specs=[block, vmem, vmem, vmem, vmem, vmem],
        out_specs=(block, vmem),
        compiler_params=pltpu.CompilerParams(vmem_limit_bytes=32 * 2**20),
        name="output",
    )(x, first, last, pe4, we4, gram)


def per_device(regressors, weights, first_week, last_week):
    pe4, we4, gram = effects(regressors, weights, first_week, last_week)
    return output(regressors, first_week, last_week, pe4, we4, gram)


def solution(mesh):
    return jax.shard_map(
        per_device,
        mesh=mesh,
        in_specs=(P(None, "week", "prod"), P("week", "prod"), P("prod"), P("prod")),
        out_specs=(P(None, "week", "prod"), P()),
        check_vma=False,
    )
```

```python
import functools

import jax
import jax.numpy as jnp
from jax import lax
from jax.experimental import pallas as pl
from jax.experimental.pallas import tpu as pltpu
from jax.sharding import PartitionSpec as P

MESH = pl.DeviceIdType.MESH
F32 = jnp.float32
BF16 = jnp.bfloat16
HI = lax.Precision.HIGHEST
NT = (((1,), (1,)), ((), ()))
NN = (((1,), (0,)), ((), ()))

K = 32
WK = 64
PD = 1536
NW = 8
NX = 4
NP = 32
WEEKS = NW * WK
LC = 384
HALF = PD // 2
W_PARTS = (0, 16, 40, 64)
R_FIRST = 8
VMEM_LIMIT = 53 * 2**20


def split3(v):
    hi = v.astype(BF16)
    r = v - hi.astype(F32)
    mid = r.astype(BF16)
    lo = (r - mid.astype(F32)).astype(BF16)
    return hi, mid, lo


def loop(lo, hi, body):
    def step(i, carry):
        body(i)
        return carry

    lax.fori_loop(lo, hi, step, 0)


class Transfer:
    def __init__(self, ds, send, arrival=None):
        self.ds, self.send, self.arrival = ds, send, arrival or send
        self.sent, self.got = [], []

    def each(self, ds, act):
        if isinstance(ds, range) and len(ds) > 3:
            loop(ds.start, ds.stop, act)
        else:
            for d in ds:
                act(d)

    def start(self, ds=None):
        ds = self.ds if ds is None else ds
        self.each(ds, lambda d: self.send(d).start())
        self.sent += list(ds)

    def wait(self, ds=None):
        ds = self.ds if ds is None else ds
        self.each(ds, lambda d: self.arrival(d).wait_recv())
        self.got += list(ds)

    def drain(self):
        self.each(self.ds if len(self.sent) == len(self.ds) else self.sent, lambda d: self.send(d).wait_send())


def effects_kernel(
    x_hbm, cell_in,
    pe4_out, we4_out, gram_out,
    x, wfull, wb, pt_own, pt_sib, pt_all, pt, wt_part, ps_stage, ps_sib, ps_recv, pe1_chunks, pe1,
    b_pack, b_y, b_z, b_all, m_stage, m_recv, mm, m_hi, m_mid, m_lo,
    q_buf, u_buf, r_pack, r_week, r_prod, we_buf,
    x_sem, pt_s, pt_r, ps_s, ps_r, wt_s, wt_r, pe_s, pe_r, pf_s, pf_r, wx_s, wx_r, wc_s, wc_r, wy_s, wy_r, wd_s, wd_r,
    by_s, by_r, bz_s, bz_r, ba_s, ba_r, ms_s, ms_r, ma_s, ma_r, mx_s, mx_r, mc_s, mc_r,
    rw_s, rw_r, rp_s, rp_r,
):
    w = lax.axis_index("week")
    p = lax.axis_index("prod")
    xi = w // 2
    core = lax.rem(w, 2)
    sib = xi * 2 + (1 - core)

    def week_peer(d):
        return lax.rem(w + d, NW)

    def prod_peer(d):
        return lax.rem(p + d, NP)

    def grid_peer(d, sign):
        y = lax.rem(p // 8 + 4 + sign * (d // 8), 4)
        z = lax.rem(lax.rem(p, 8) + 8 + sign * (d % 8), 8)
        return y * 8 + z

    def x_peer(d):
        return lax.rem(xi + d, NX) * 2 + core

    def x_from(d):
        return lax.rem(xi + NX - d, NX) * 2 + core

    def to_week(src, dst, ssem, rsem, q):
        return pltpu.make_async_remote_copy(
            src_ref=src, dst_ref=dst, send_sem=ssem, recv_sem=rsem,
            device_id={"week": q}, device_id_type=MESH,
        )

    def to_prod(src, dst, ssem, rsem, q):
        return pltpu.make_async_remote_copy(
            src_ref=src, dst_ref=dst, send_sem=ssem, recv_sem=rsem,
            device_id={"prod": q}, device_id_type=MESH,
        )

    def x_copy(c):
        rows = pl.ds(c * 8, 8)
        return pltpu.make_async_copy(x_hbm.at[rows], x.at[rows], x_sem.at[c])

    for c in range(4):
        x_copy(c).start()

    barrier = pltpu.get_barrier_semaphore()

    def greet_week(d):
        pl.semaphore_signal(barrier, inc=1, device_id={"week": week_peer(d)}, device_id_type=MESH)

    def greet_prod(d):
        pl.semaphore_signal(barrier, inc=1, device_id={"prod": prod_peer(d)}, device_id_type=MESH)

    loop(1, NW, greet_week)
    loop(1, NP, greet_prod)

    cell = cell_in[...]
    wfull[w] = cell
    wb[pl.ds(pl.multiple_of(w * WK, WK), WK), :] = cell.astype(BF16)
    pt_own[...] = jnp.sum(cell, axis=0, keepdims=True)
    lane = lax.broadcasted_iota(jnp.int32, (WK, 128), 1)
    row = lax.broadcasted_iota(jnp.int32, (WK, 128), 0)
    wt_col = jnp.sum(cell, axis=1, keepdims=True)
    wt_part[p] = jnp.sum(jnp.where(lane == row, wt_col, 0.0), axis=0, keepdims=True)

    def sums_group(g, acc):
        x_copy(g).wait()

        def one(j, acc):
            k = g * 8 + j
            part = jnp.zeros((WK, 128), F32)
            for c in range(PD // LC):
                lanes = slice(c * LC, (c + 1) * LC)
                weighted = x[k, :, lanes].astype(F32) * wfull[w, :, lanes]
                half, off = c // 2, (c % 2) * LC
                ps_stage[half, g, pl.ds(j, 1), off:off + LC] = jnp.sum(weighted, axis=0, keepdims=True)
                for t in range(LC // 128):
                    part = part + weighted[:, t * 128:(t + 1) * 128]
            return acc + jnp.where(lane == k, jnp.sum(part, axis=1, keepdims=True), 0.0)

        return lax.fori_loop(0, 8, one, acc, unroll=2)

    ws = lax.fori_loop(0, 4, sums_group, jnp.zeros((WK, 128), F32))

    pl.semaphore_wait(barrier, NW - 1 + NP - 1)

    def pt_copy(d):
        if d == 0:
            return to_week(pt_own, pt_sib, pt_s.at[0], pt_r.at[0], sib)
        return to_week(pt_all.at[xi], pt_all.at[xi], pt_s.at[d], pt_r.at[d], x_peer(d))

    def pt_arrived(d):
        if d == 0:
            return pt_copy(0)
        return to_week(pt_all.at[xi], pt_all.at[lax.rem(xi + NX - d, NX)], pt_s.at[d], pt_r.at[d], x_peer(d))

    def ps_copy(d):
        if d == 0:
            return to_week(ps_stage.at[1 - core], ps_sib, ps_s.at[0], ps_r.at[0], sib)
        q = x_peer(d)
        return to_week(ps_stage.at[core, lax.rem(xi + d, NX)], ps_recv.at[d], ps_s.at[d], ps_r.at[d], q)

    pt_move = Transfer((0, 2, 1, 3), pt_copy, pt_arrived)
    ps_move = Transfer((0, 2, 1, 3), ps_copy)
    pt_move.start((0,))
    ps_move.start((0,))

    def wt_copy(d):
        return to_prod(wt_part.at[p], wt_part.at[p], wt_s.at[d], wt_r.at[d], prod_peer(d))

    def wt_arrived(d):
        return to_prod(wt_part.at[p], wt_part.at[lax.rem(p + NP - d, NP)], wt_s.at[d], wt_r.at[d], prod_peer(d))

    def first_half(chip, other):
        return jnp.where(chip < other, 0, 1)

    def half_of(slot, h):
        return wfull.at[slot, :, pl.ds(pl.multiple_of(h * HALF, HALF), HALF)]

    def chip_to(d):
        return lax.rem(xi + d, NX)

    def chip_from(d):
        return lax.rem(xi + NX - d, NX)

    def part_of(slot, h, e):
        lo, hi = W_PARTS[e], W_PARTS[e + 1]
        return wfull.at[slot, pl.ds(lo, hi - lo), pl.ds(pl.multiple_of(h * HALF, HALF), HALF)]

    def wx_copy(i):
        d, e = i % NX, i // NX
        h = first_half(chip_to(d), xi)
        return to_week(part_of(w, h, e), part_of(w, h, e), wx_s.at[i], wx_r.at[i], x_peer(d))

    def wx_arrived(i):
        d, e = i % NX, i // NX
        h = first_half(xi, chip_from(d))
        return to_week(part_of(w, h, e), part_of(x_from(d), h, e), wx_s.at[i], wx_r.at[i], x_peer(d))

    def wy_copy(d):
        h = 1 - first_half(chip_to(d), xi)
        return to_week(half_of(w, h), half_of(w, h), wy_s.at[d], wy_r.at[d], x_peer(d))

    def wy_arrived(d):
        h = 1 - first_half(xi, chip_from(d))
        return to_week(half_of(w, h), half_of(x_from(d), h), wy_s.at[d], wy_r.at[d], x_peer(d))

    def other_core(slot):
        return slot + 1 - 2 * core

    def wc_copy(i):
        d, e = i % NX, i // NX
        if d == 0:
            return to_week(wfull.at[w], wfull.at[w], wc_s.at[i], wc_r.at[i], sib)
        here = part_of(x_from(d), first_half(xi, chip_from(d)), e)
        return to_week(here, here, wc_s.at[i], wc_r.at[i], sib)

    def wc_arrived(i):
        d, e = i % NX, i // NX
        if d == 0:
            return to_week(wfull.at[w], wfull.at[sib], wc_s.at[i], wc_r.at[i], sib)
        here = part_of(other_core(x_from(d)), first_half(xi, chip_from(d)), e)
        return to_week(here, here, wc_s.at[i], wc_r.at[i], sib)

    def wd_copy(d):
        here = half_of(x_from(d), 1 - first_half(xi, chip_from(d)))
        return to_week(here, here, wd_s.at[d], wd_r.at[d], sib)

    def wd_arrived(d):
        here = half_of(other_core(x_from(d)), 1 - first_half(xi, chip_from(d)))
        return to_week(here, here, wd_s.at[d], wd_r.at[d], sib)

    wt_move = Transfer(range(1, NP), wt_copy, wt_arrived)
    wt_move.start()
    parts = range(len(W_PARTS) - 1)
    wx_move = Transfer([d + NX * e for e in parts for d in (2, 1, 3)], wx_copy, wx_arrived)
    wc_move = Transfer([0] + [d + NX * e for e in parts for d in (1, 3, 2)], wc_copy, wc_arrived)
    wy_move = Transfer((2, 1, 3), wy_copy, wy_arrived)
    wd_move = Transfer((1, 3, 2), wd_copy, wd_arrived)

    def send_part(e):
        wx_move.start([d + NX * e for d in (2, 1, 3)])

    send_part(0)
    pt_move.wait((0,))
    pt_all[xi] = pt_own[...] + pt_sib[...]
    ps_move.wait((0,))
    for a in range(NX):
        ps_stage[core, a] = ps_stage[core, a] + ps_sib[a]
    pt_move.start((2, 1, 3))
    ps_move.start((2, 1, 3))
    wc_move.start((0,))
    send_part(1)
    pt_move.wait((2, 1, 3))
    ps_move.wait((2, 1, 3))
    pt[...] = jnp.sum(pt_all[...], axis=0)
    total = ps_stage[core, xi]
    for d in range(1, NX):
        total = total + ps_recv[d]
    own_half = pl.ds(pl.multiple_of(core * HALF, HALF), HALF)
    pe1_chunks[w] = total / pt[:, own_half]

    def pe_copy(d):
        return to_week(pe1_chunks.at[w], pe1_chunks.at[w], pe_s.at[d], pe_r.at[d], x_peer(d))

    def pe_arrived(d):
        return to_week(pe1_chunks.at[w], pe1_chunks.at[x_from(d)], pe_s.at[d], pe_r.at[d], x_peer(d))

    def pf_copy(d):
        slot = x_from(d)
        return to_week(pe1_chunks.at[slot], pe1_chunks.at[slot], pf_s.at[d], pf_r.at[d], sib)

    def pf_arrived(d):
        slot = other_core(x_from(d))
        return to_week(pe1_chunks.at[slot], pe1_chunks.at[slot], pf_s.at[d], pf_r.at[d], sib)

    pe_move = Transfer((2, 1, 3), pe_copy, pe_arrived)
    pf_move = Transfer((0, 1, 3, 2), pf_copy, pf_arrived)
    pe_move.start()
    pf_move.start((0,))
    for e in parts[2:]:
        send_part(e)

    def wb_half(slot, h):
        return wb.at[
            pl.ds(pl.multiple_of(slot * WK, WK), WK),
            pl.ds(pl.multiple_of(h * HALF, HALF), HALF),
        ]

    for e in parts[:2]:
        for d in (1, 3, 2):
            wx_move.wait((d + NX * e,))
            wc_move.start((d + NX * e,))

    for d in (1, 3, 2):
        pe_move.wait((d,))
        pf_move.start((d,))
    pf_move.wait()
    for r in range(NW):
        pe1[(r // 2) * 8:(r // 2) * 8 + 8, (r % 2) * HALF:(r % 2 + 1) * HALF] = pe1_chunks[r]
    hi, mid, lo = split3(pe1[...])
    pe_rows = jnp.concatenate([hi, mid, lo, jnp.zeros((K, PD), BF16)], axis=0)
    own_wb = wb[pl.ds(pl.multiple_of(w * WK, WK), WK), :]
    taken = lax.dot_general(own_wb, pe_rows, NT, preferred_element_type=F32)
    taken = taken + (pltpu.roll(taken, 128 - K, 1) + pltpu.roll(taken, 128 - 2 * K, 1))
    bt = jnp.where(lane < K, ws - taken, 0.0)
    b_pack[0] = sum(
        [pltpu.roll(bt[16 * a:16 * a + 16], 32 * a, 1) for a in range(1, 4)], bt[:16]
    )

    def by_copy(d):
        return to_prod(b_pack.at[0], b_y.at[d], by_s.at[d], by_r.at[d], grid_peer(8 * d, 1))

    def bz_copy(d):
        return to_prod(b_pack.at[1], b_z.at[d], bz_s.at[d], bz_r.at[d], grid_peer(d, 1))

    by_move = Transfer((2, 1, 3), by_copy)
    bz_move = Transfer((4, 3, 5, 2, 6, 1, 7), bz_copy)
    by_move.start()

    for e in parts[2:]:
        for d in (1, 3, 2):
            wx_move.wait((d + NX * e,))
            wc_move.start((d + NX * e,))
    wy_move.start()
    by_move.wait()
    b_pack[1] = (b_pack[0] + b_y[1]) + (b_y[2] + b_y[3])
    bz_move.start()
    hi, mid, lo = split3(wfull[w] / pt[...])
    wc_move.wait()

    for h in (0, 1):
        wb_half(sib, h)[...] = half_of(sib, h)[...].astype(BF16)

    def to_bf16(i):
        d = 1 + i // 2
        slot = chip_from(d) * 2 + lax.rem(i, 2)
        h = first_half(xi, chip_from(d))
        wb_half(slot, h)[...] = half_of(slot, h)[...].astype(BF16)
        wb_half(slot, 1 - h)[...] = jnp.zeros((WK, HALF), BF16)

    loop(0, NW - 2, to_bf16)
    rows = jnp.concatenate([hi, mid, lo], axis=0)
    m3 = lax.dot_general(rows, wb[...], NT, preferred_element_type=F32)
    m_own = m3[:WK] + (m3[WK:2 * WK] + m3[2 * WK:])
    for q in range(NP):
        m_stage[q] = m_own[(q // 4) * 8:(q // 4) * 8 + 8, (q % 4) * 128:(q % 4 + 1) * 128]

    def ms_copy(d):
        q = prod_peer(d)
        return to_prod(m_stage.at[q], m_recv.at[d], ms_s.at[d], ms_r.at[d], q)

    ms_move = Transfer(range(1, NP), ms_copy)
    ms_move.start()

    bz_move.wait()
    wt_move.wait()
    wt_row = lax.fori_loop(0, NP, lambda d, a: a + wt_part[d], jnp.zeros((1, 128), F32))
    wt_own = jnp.sum(jnp.where(lane == row, wt_row, 0.0), axis=1, keepdims=True)
    packed = sum([b_z[d] for d in range(1, 8)], b_pack[1])
    b_own = jnp.concatenate(
        [packed] + [pltpu.roll(packed, 128 - 32 * a, 1) for a in range(1, 4)], axis=0
    )
    b_own = jnp.where(lane < K, b_own, jnp.where(lane == K, wt_own, 0.0))
    b_all[w] = b_own[:32] + pltpu.roll(b_own[32:], 64, 1)
    own_rows = pl.ds(pl.multiple_of(w * WK, WK), WK)

    def ba_copy(d):
        return to_week(b_all.at[w], b_all.at[w], ba_s.at[d], ba_r.at[d], week_peer(d))

    def ba_arrived(d):
        return to_week(b_all.at[w], b_all.at[lax.rem(w + NW - d, NW)], ba_s.at[d], ba_r.at[d], week_peer(d))

    ba_move = Transfer(range(1, NW), ba_copy, ba_arrived)
    ba_move.start()

    we_buf[pl.ds(0, WK), :] = b_own / wt_own

    def r_pair(j):
        we1 = we_buf[pl.ds(0, WK), :]
        cols = [
            jnp.sum(jnp.where(lane == 2 * j + e, we1, 0.0), axis=1, keepdims=True)
            for e in range(2)
        ]
        at = pl.ds(pl.multiple_of(j * 16, 16), 16)
        for c in range(PD // 256):
            lanes = slice(c * 256, (c + 1) * 256)
            cellw = wfull[w, :, lanes]
            fs = []
            for e in range(2):
                k = 2 * j + e
                f = x[k, :, lanes].astype(F32) - pe1[pl.ds(k, 1), lanes] - cols[e]
                fs.append(f)
            for g in range(8):
                s = slice(g * 8, g * 8 + 8)
                pair = jnp.concatenate([fs[0][s], fs[1][s]], axis=0)
                wpair = jnp.concatenate([fs[0][s] * cellw[s], fs[1][s] * cellw[s]], axis=0)
                q_buf[g, at, lanes] = pair.astype(BF16)
                u_buf[g, at, lanes] = wpair.astype(BF16)

    loop(0, R_FIRST, r_pair)

    ms_move.wait()
    tile = lax.fori_loop(1, NP, lambda d, a: a + m_recv[d], m_stage[p])

    def tile_of(wk, q):
        return mm.at[
            pl.ds(pl.multiple_of(wk * WK + (q // 4) * 8, 8), 8),
            pl.ds(pl.multiple_of(lax.rem(q, 4) * 128, 128), 128),
        ]

    tile_of(w, p)[...] = tile

    def ma_copy(d):
        return to_prod(tile_of(w, p), tile_of(w, p), ma_s.at[d], ma_r.at[d], grid_peer(d, 1))

    def ma_arrived(d):
        return to_prod(tile_of(w, p), tile_of(w, grid_peer(d, -1)), ma_s.at[d], ma_r.at[d], grid_peer(d, 1))

    def forward_tile(q):
        for d in (2, 1, 3):
            to_week(tile_of(w, q), tile_of(w, q), mx_s.at[d], mx_r.at[d], x_peer(d)).start()

    near_first = sorted(
        range(1, NP), key=lambda d: min(d // 8, 4 - d // 8) + min(d % 8, 8 - d % 8)
    )
    ma_move = Transfer(near_first, ma_copy, ma_arrived)
    ma_move.start(near_first[::-1])
    forward_tile(p)

    for d in (1, 3, 2):
        wy_move.wait((d,))
        wd_move.start((d,))

    def r_dot(g, acc):
        return acc + lax.dot_general(u_buf[g], q_buf[g], NT, preferred_element_type=F32)

    def forward_tiles(ds):
        for d in ds:
            ma_move.wait((d,))
            forward_tile(grid_peer(d, -1))

    loop(R_FIRST, K // 2, r_pair)
    big = lax.fori_loop(0, 5, r_dot, jnp.zeros((K * 8, K * 8), F32))
    forward_tiles(near_first[:6])
    big = lax.fori_loop(5, 7, r_dot, big)
    forward_tiles(near_first[6:14])
    big = r_dot(7, big)
    ri = lax.broadcasted_iota(jnp.int32, (K * 8, K * 8), 0)
    ci = lax.broadcasted_iota(jnp.int32, (K * 8, K * 8), 1)
    big = jnp.where(lax.rem(ri, 8) == lax.rem(ci, 8), big, 0.0)
    ei = lax.broadcasted_iota(jnp.int32, (K, K * 8), 0)
    ej = lax.broadcasted_iota(jnp.int32, (K, K * 8), 1)
    fold = jnp.where(ei == ej // 8, 1.0, 0.0)
    fi = lax.broadcasted_iota(jnp.int32, (K * 8, 128), 0)
    fj = lax.broadcasted_iota(jnp.int32, (K * 8, 128), 1)
    fold_t = jnp.where(fi // 8 == fj, 1.0, 0.0)
    half_done = lax.dot_general(fold, big, NN, precision=HI, preferred_element_type=F32)
    r2 = lax.dot_general(half_done, fold_t, NN, precision=HI, preferred_element_type=F32)
    r_pack[0] = r2[0:8] + pltpu.roll(r2[8:16], 32, 1) + pltpu.roll(r2[16:24], 64, 1) + pltpu.roll(r2[24:32], 96, 1)

    def rw_copy(d):
        return to_week(r_pack.at[0], r_week.at[d], rw_s.at[d], rw_r.at[d], week_peer(d))

    rw_move = Transfer(range(1, NW), rw_copy)
    rw_move.start()

    forward_tiles(near_first[14:])

    def rows_of(wk):
        return mm.at[pl.ds(pl.multiple_of(wk * WK, WK), WK)]

    def mx_copy(d):
        return to_week(rows_of(w), rows_of(w), mx_s.at[d], mx_r.at[d], x_peer(d))

    def mx_arrived(d):
        return to_week(rows_of(w), rows_of(x_from(d)), mx_s.at[d], mx_r.at[d], x_peer(d))

    def mc_copy(d):
        slot = x_from(d)
        return to_week(rows_of(slot), rows_of(slot), mc_s.at[d], mc_r.at[d], sib)

    def mc_arrived(d):
        slot = x_from(d) + 1 - 2 * core
        return to_week(rows_of(slot), rows_of(slot), mc_s.at[d], mc_r.at[d], sib)

    mx_move = Transfer((1, 3, 2), mx_copy, mx_arrived)
    mc_move = Transfer((0, 1, 3, 2), mc_copy, mc_arrived)
    mx_move.sent += [1, 3, 2]
    mc_move.start((0,))

    rw_move.wait()
    r_sum = r_pack[0]
    for d in range(1, NW):
        r_sum = r_sum + r_week[d]
    r_pack[1] = r_sum

    def rp_copy(d):
        return to_prod(r_pack.at[1], r_prod.at[d], rp_s.at[d], rp_r.at[d], prod_peer(d))

    rp_move = Transfer(range(1, NP), rp_copy)
    rp_move.start()
    for d in (1, 3, 2):
        mx_move.wait((d,))
        mc_move.start((d,))
    wd_move.wait()

    def rest_to_bf16(i):
        d = 1 + i // 2
        slot = chip_from(d) * 2 + lax.rem(i, 2)
        h = 1 - first_half(xi, chip_from(d))
        wb_half(slot, h)[...] = half_of(slot, h)[...].astype(BF16)

    loop(0, NW - 2, rest_to_bf16)

    ba_move.wait()
    lane_all = lax.broadcasted_iota(jnp.int32, (WEEKS, 128), 1)
    pieces = []
    for i in range(NW):
        piece = b_all[i]
        pieces += [piece, pltpu.roll(piece, 64, 1)]
    b = jnp.concatenate(pieces, axis=0)
    wt = jnp.sum(jnp.where(lane_all == K, b, 0.0), axis=1, keepdims=True)
    b = jnp.where(lane_all < K, b, 0.0)
    we1 = b / wt
    weight_total = jnp.sum(wt, axis=0, keepdims=True)

    mc_move.wait()

    def put_m(rows, cols, v):
        hi, mid, lo = split3(v)
        m_hi[rows, cols] = hi
        m_mid[rows, cols] = mid
        m_lo[rows, cols] = lo

    blocks = [slice(a * 128, a * 128 + 128) for a in range(NX)]
    for a in range(NX):
        put_m(blocks[a], blocks[a], mm[blocks[a], blocks[a]])
        for c in range(a + 1, NX):
            both = mm[blocks[a], blocks[c]] + mm[blocks[c], blocks[a]].T
            put_m(blocks[a], blocks[c], both)
            put_m(blocks[c], blocks[a], both.T)

    def apply_m(v):
        hi, mid, lo = [part.astype(F32) for part in split3(v)]
        parts = (hi + pltpu.roll(mid, K, 1) + pltpu.roll(lo, 2 * K, 1)).astype(BF16)
        acc = jnp.dot(m_hi[...], parts, preferred_element_type=F32)
        acc = acc + jnp.where(lane_all < 2 * K, jnp.dot(m_mid[...], parts, preferred_element_type=F32), 0.0)
        acc = acc + jnp.where(lane_all < K, jnp.dot(m_lo[...], parts, preferred_element_type=F32), 0.0)
        acc = acc + (pltpu.roll(acc, 128 - K, 1) + pltpu.roll(acc, 128 - 2 * K, 1))
        return jnp.where(lane_all < K, acc, 0.0)

    n1 = apply_m(we1)
    we2 = (b + n1) / wt
    we3 = (b + apply_m(we2)) / wt
    n3 = apply_m(we3)
    we4 = (b + n3) / wt
    we_buf[...] = we4
    we4_out[...] = we_buf[own_rows, :]

    we3_t = we3.T[:K]
    hi, mid, lo = split3(we3_t)
    rows = jnp.concatenate([hi, mid, lo], axis=0)
    wp3 = lax.dot_general(rows, wb[...], NN, preferred_element_type=F32)
    wp = wp3[:K] + (wp3[K:2 * K] + wp3[2 * K:])
    pe4_out[...] = pe1[...] - wp / pt[...]

    rp_move.wait()
    r_total = lax.fori_loop(1, NP, lambda d, a: a + r_prod[d], r_pack[1])
    gram = lax.dot_general((we3 - we4).T[:K], n3, NN, precision=HI, preferred_element_type=F32)
    gram = gram - lax.dot_general(we3_t, n1, NN, precision=HI, preferred_element_type=F32)
    r_rows = jnp.concatenate(
        [r_total] + [pltpu.roll(r_total, 128 - 32 * a, 1) for a in range(1, 4)], axis=0
    )
    gram_out[...] = ((r_rows + gram) / weight_total)[:, :K]

    for move in (
        pt_move, ps_move, wt_move, wx_move, wc_move, wy_move, wd_move, pe_move, pf_move, by_move, bz_move, ba_move,
        ms_move, ma_move, mx_move, mc_move, rw_move, rp_move,
    ):
        move.drain()


def effects(x, cell):
    vmem = pl.BlockSpec(memory_space=pltpu.VMEM)
    dma = pltpu.SemaphoreType.DMA
    scratch = [
        pltpu.VMEM((K, WK, PD), BF16),
        pltpu.VMEM((NW, WK, PD), F32),
        pltpu.VMEM((WEEKS, PD), BF16),
        pltpu.VMEM((1, PD), F32),
        pltpu.VMEM((1, PD), F32),
        pltpu.VMEM((NX, 1, PD), F32),
        pltpu.VMEM((1, PD), F32),
        pltpu.VMEM((NP, 1, 128), F32),
        pltpu.VMEM((2, NX, 8, HALF), F32),
        pltpu.VMEM((NX, 8, HALF), F32),
        pltpu.VMEM((NX, 8, HALF), F32),
        pltpu.VMEM((NW, 8, HALF), F32),
        pltpu.VMEM((K, PD), F32),
        pltpu.VMEM((2, 16, 128), F32),
        pltpu.VMEM((4, 16, 128), F32),
        pltpu.VMEM((8, 16, 128), F32),
        pltpu.VMEM((NW, 32, 128), F32),
        pltpu.VMEM((NP, 8, 128), F32),
        pltpu.VMEM((NP, 8, 128), F32),
        pltpu.VMEM((WEEKS, WEEKS), F32),
        pltpu.VMEM((WEEKS, WEEKS), BF16),
        pltpu.VMEM((WEEKS, WEEKS), BF16),
        pltpu.VMEM((WEEKS, WEEKS), BF16),
        pltpu.VMEM((8, K * 8, PD), BF16),
        pltpu.VMEM((8, K * 8, PD), BF16),
        pltpu.VMEM((2, 8, 128), F32),
        pltpu.VMEM((NW, 8, 128), F32),
        pltpu.VMEM((NP, 8, 128), F32),
        pltpu.VMEM((WEEKS, 128), F32),
        dma((4,)),
    ]
    for n in (NX, NX, NP, NX, NX, len(W_PARTS) * NX, len(W_PARTS) * NX, NX, NX, 4, 8, NW, NP, NP, NX, NX, NW, NP):
        scratch += [dma((n,)), dma((n,))]
    return pl.pallas_call(
        effects_kernel,
        out_shape=(
            jax.ShapeDtypeStruct((K, PD), F32),
            jax.ShapeDtypeStruct((WK, 128), F32),
            jax.ShapeDtypeStruct((K, K), F32),
        ),
        in_specs=[pl.BlockSpec(memory_space=pl.ANY), vmem],
        out_specs=(vmem, vmem, vmem),
        scratch_shapes=scratch,
        compiler_params=pltpu.CompilerParams(
            collective_id=0, has_side_effects=True, vmem_limit_bytes=VMEM_LIMIT
        ),
        name="effects",
    )(x, cell)


KB = 4


def output_kernel(x, cell, pe4, we4, gram, out_hbm, gram_out, out, sem):
    gram_out[...] = gram[...]
    lane = lax.broadcasted_iota(jnp.int32, (WK, 128), 1)

    def copy(i):
        rows = pl.ds(i * KB, KB)
        return pltpu.make_async_copy(out.at[rows], out_hbm.at[rows], sem.at[i])

    def block(i):
        for e in range(KB):
            k = i * KB + e
            col = jnp.sum(jnp.where(lane == k, we4[...], 0.0), axis=1, keepdims=True)
            for c in range(PD // LC):
                lanes = slice(c * LC, (c + 1) * LC)
                field = x[k, :, lanes].astype(F32) - pe4[pl.ds(k, 1), lanes] - col
                out[k, :, lanes] = jnp.where(cell[:, lanes] > 0.0, field, 0.0).astype(BF16)
        copy(i).start()

    loop(0, K // KB, block)
    loop(0, K // KB, lambda i: copy(i).wait())


def output(x, cell, pe4, we4, gram):
    vmem = pl.BlockSpec(memory_space=pltpu.VMEM)
    return pl.pallas_call(
        output_kernel,
        out_shape=(
            jax.ShapeDtypeStruct((K, WK, PD), BF16),
            jax.ShapeDtypeStruct((K, K), F32),
        ),
        in_specs=[vmem] * 5,
        out_specs=(pl.BlockSpec(memory_space=pl.ANY), vmem),
        scratch_shapes=[pltpu.VMEM((K, WK, PD), BF16), pltpu.SemaphoreType.DMA((K // KB,))],
        compiler_params=pltpu.CompilerParams(vmem_limit_bytes=32 * 2**20),
        name="output",
    )(x, cell, pe4, we4, gram)


def per_device(regressors, weights, first_week, last_week):
    ids = lax.axis_index("week") * WK + lax.broadcasted_iota(jnp.int32, (WK, PD), 0)
    live = (ids >= first_week[None, :]) & (ids <= last_week[None, :])
    cell = jnp.where(live, weights.astype(F32), 0.0)
    pe4, we4, gram = effects(regressors, cell)
    return output(regressors, cell, pe4, we4, gram)


def solution(mesh):
    return jax.shard_map(
        per_device,
        mesh=mesh,
        in_specs=(P(None, "week", "prod"), P("week", "prod"), P("prod"), P("prod")),
        out_specs=(P(None, "week", "prod"), P()),
        check_vma=False,
    )
```

```python
import functools

import jax
import jax.numpy as jnp
from jax import lax
from jax.experimental import pallas as pl
from jax.experimental.pallas import tpu as pltpu
from jax.sharding import PartitionSpec as P

MESH = pl.DeviceIdType.MESH
F32 = jnp.float32
BF16 = jnp.bfloat16
HI = lax.Precision.HIGHEST
NT = (((1,), (1,)), ((), ()))
NN = (((1,), (0,)), ((), ()))

K = 32
WK = 64
PD = 1536
NW = 8
NX = 4
NP = 32
WEEKS = NW * WK
LC = 384
HALF = PD // 2
W_PARTS = (0, 8, 40, 64)
R_FIRST = 4
VMEM_LIMIT = 53 * 2**20


def split3(v):
    hi = v.astype(BF16)
    r = v - hi.astype(F32)
    mid = r.astype(BF16)
    lo = (r - mid.astype(F32)).astype(BF16)
    return hi, mid, lo


def loop(lo, hi, body):
    def step(i, carry):
        body(i)
        return carry

    lax.fori_loop(lo, hi, step, 0)


class Transfer:
    def __init__(self, ds, send, arrival=None):
        self.ds, self.send, self.arrival = ds, send, arrival or send
        self.sent, self.got = [], []

    def each(self, ds, act):
        if isinstance(ds, range) and len(ds) > 3:
            loop(ds.start, ds.stop, act)
        else:
            for d in ds:
                act(d)

    def start(self, ds=None):
        ds = self.ds if ds is None else ds
        self.each(ds, lambda d: self.send(d).start())
        self.sent += list(ds)

    def wait(self, ds=None):
        ds = self.ds if ds is None else ds
        self.each(ds, lambda d: self.arrival(d).wait_recv())
        self.got += list(ds)

    def drain(self):
        self.each(self.ds if len(self.sent) == len(self.ds) else self.sent, lambda d: self.send(d).wait_send())


def effects_kernel(
    x_hbm, cell_in,
    pe4_out, we4_out, gram_out,
    x, wfull, wb, pt_own, pt_sib, pt_all, pt, ps_stage, ps_sib, ps_recv, pe1_chunks, pe1,
    b_pack, b_y, b_z, b_all, m_stage, m_recv, mm, m_hi, m_mid, m_lo,
    q_buf, u_buf, r_pack, r_week, r_prod, we_buf,
    x_sem, ready, pt_s, pt_r, ps_s, ps_r, pe_s, pe_r, pf_s, pf_r, wx_s, wx_r, wc_s, wc_r, wy_s, wy_r, wd_s, wd_r,
    by_s, by_r, bz_s, bz_r, ba_s, ba_r, ms_s, ms_r, ma_s, ma_r, mx_s, mx_r, mc_s, mc_r,
    rw_s, rw_r, rp_s, rp_r,
):
    w = lax.axis_index("week")
    p = lax.axis_index("prod")
    xi = w // 2
    core = lax.rem(w, 2)
    sib = xi * 2 + (1 - core)

    def week_peer(d):
        return lax.rem(w + d, NW)

    def prod_peer(d):
        return lax.rem(p + d, NP)

    def grid_peer(d, sign):
        y = lax.rem(p // 8 + 4 + sign * (d // 8), 4)
        z = lax.rem(lax.rem(p, 8) + 8 + sign * (d % 8), 8)
        return y * 8 + z

    def x_peer(d):
        return lax.rem(xi + d, NX) * 2 + core

    def x_from(d):
        return lax.rem(xi + NX - d, NX) * 2 + core

    def to_week(src, dst, ssem, rsem, q):
        return pltpu.make_async_remote_copy(
            src_ref=src, dst_ref=dst, send_sem=ssem, recv_sem=rsem,
            device_id={"week": q}, device_id_type=MESH,
        )

    def to_prod(src, dst, ssem, rsem, q):
        return pltpu.make_async_remote_copy(
            src_ref=src, dst_ref=dst, send_sem=ssem, recv_sem=rsem,
            device_id={"prod": q}, device_id_type=MESH,
        )

    def x_copy(c):
        rows = pl.ds(c * 8, 8)
        return pltpu.make_async_copy(x_hbm.at[rows], x.at[rows], x_sem.at[c])

    for c in range(4):
        x_copy(c).start()

    barrier = pltpu.get_barrier_semaphore()

    def greet_week(d):
        pl.semaphore_signal(barrier, inc=1, device_id={"week": week_peer(d)}, device_id_type=MESH)

    def greet_grid(d):
        pl.semaphore_signal(barrier, inc=1, device_id={"prod": grid_peer(d, 1)}, device_id_type=MESH)

    loop(1, NW, greet_week)
    loop(1, 4, lambda d: greet_grid(8 * d))
    loop(1, 8, greet_grid)

    cell = cell_in[...]
    wfull[w] = cell
    wb[pl.ds(pl.multiple_of(w * WK, WK), WK), :] = cell.astype(BF16)
    pt_own[...] = jnp.sum(cell, axis=0, keepdims=True)
    lane = lax.broadcasted_iota(jnp.int32, (WK, 128), 1)
    row = lax.broadcasted_iota(jnp.int32, (WK, 128), 0)
    wt_col = jnp.sum(cell, axis=1, keepdims=True)
    wt_local = jnp.sum(jnp.where(lane == row, wt_col, 0.0), axis=0, keepdims=True)

    def sums_group(g, acc):
        x_copy(g).wait()

        def one(j, acc):
            k = g * 8 + j
            part = jnp.zeros((WK, 128), F32)
            for c in range(PD // LC):
                lanes = slice(c * LC, (c + 1) * LC)
                weighted = x[k, :, lanes].astype(F32) * wfull[w, :, lanes]
                half, off = c // 2, (c % 2) * LC
                ps_stage[half, g, pl.ds(j, 1), off:off + LC] = jnp.sum(weighted, axis=0, keepdims=True)
                for t in range(LC // 128):
                    part = part + weighted[:, t * 128:(t + 1) * 128]
            return acc + jnp.where(lane == k, jnp.sum(part, axis=1, keepdims=True), 0.0)

        return lax.fori_loop(0, 8, one, acc, unroll=8)

    ws = lax.fori_loop(0, 4, sums_group, jnp.zeros((WK, 128), F32))

    pl.semaphore_wait(barrier, NW - 1 + 3 + 7)

    def pass_on(d):
        pl.semaphore_signal(ready, inc=1, device_id={"prod": grid_peer(d, 1)}, device_id_type=MESH)

    loop(1, 8, pass_on)

    def pt_copy(d):
        if d == 0:
            return to_week(pt_own, pt_sib, pt_s.at[0], pt_r.at[0], sib)
        return to_week(pt_all.at[xi], pt_all.at[xi], pt_s.at[d], pt_r.at[d], x_peer(d))

    def pt_arrived(d):
        if d == 0:
            return pt_copy(0)
        return to_week(pt_all.at[xi], pt_all.at[lax.rem(xi + NX - d, NX)], pt_s.at[d], pt_r.at[d], x_peer(d))

    def ps_copy(d):
        if d == 0:
            return to_week(ps_stage.at[1 - core], ps_sib, ps_s.at[0], ps_r.at[0], sib)
        q = x_peer(d)
        return to_week(ps_stage.at[core, lax.rem(xi + d, NX)], ps_recv.at[d], ps_s.at[d], ps_r.at[d], q)

    pt_move = Transfer((0, 2, 1, 3), pt_copy, pt_arrived)
    ps_move = Transfer((0, 2, 1, 3), ps_copy)
    pt_move.start((0,))
    ps_move.start((0,))

    def first_half(chip, other):
        return jnp.where(chip < other, 0, 1)

    def half_of(slot, h):
        return wfull.at[slot, :, pl.ds(pl.multiple_of(h * HALF, HALF), HALF)]

    def chip_to(d):
        return lax.rem(xi + d, NX)

    def chip_from(d):
        return lax.rem(xi + NX - d, NX)

    def part_of(slot, h, e):
        lo, hi = W_PARTS[e], W_PARTS[e + 1]
        return wfull.at[slot, pl.ds(lo, hi - lo), pl.ds(pl.multiple_of(h * HALF, HALF), HALF)]

    def wx_copy(i):
        d, e = i % NX, i // NX
        h = first_half(chip_to(d), xi)
        return to_week(part_of(w, h, e), part_of(w, h, e), wx_s.at[i], wx_r.at[i], x_peer(d))

    def wx_arrived(i):
        d, e = i % NX, i // NX
        h = first_half(xi, chip_from(d))
        return to_week(part_of(w, h, e), part_of(x_from(d), h, e), wx_s.at[i], wx_r.at[i], x_peer(d))

    def wy_copy(d):
        h = 1 - first_half(chip_to(d), xi)
        return to_week(half_of(w, h), half_of(w, h), wy_s.at[d], wy_r.at[d], x_peer(d))

    def wy_arrived(d):
        h = 1 - first_half(xi, chip_from(d))
        return to_week(half_of(w, h), half_of(x_from(d), h), wy_s.at[d], wy_r.at[d], x_peer(d))

    def other_core(slot):
        return slot + 1 - 2 * core

    def wc_copy(i):
        d, e = i % NX, i // NX
        if d == 0:
            return to_week(wfull.at[w], wfull.at[w], wc_s.at[i], wc_r.at[i], sib)
        here = part_of(x_from(d), first_half(xi, chip_from(d)), e)
        return to_week(here, here, wc_s.at[i], wc_r.at[i], sib)

    def wc_arrived(i):
        d, e = i % NX, i // NX
        if d == 0:
            return to_week(wfull.at[w], wfull.at[sib], wc_s.at[i], wc_r.at[i], sib)
        here = part_of(other_core(x_from(d)), first_half(xi, chip_from(d)), e)
        return to_week(here, here, wc_s.at[i], wc_r.at[i], sib)

    def wd_copy(d):
        here = half_of(x_from(d), 1 - first_half(xi, chip_from(d)))
        return to_week(here, here, wd_s.at[d], wd_r.at[d], sib)

    def wd_arrived(d):
        here = half_of(other_core(x_from(d)), 1 - first_half(xi, chip_from(d)))
        return to_week(here, here, wd_s.at[d], wd_r.at[d], sib)

    parts = range(len(W_PARTS) - 1)
    wx_move = Transfer([d + NX * e for e in parts for d in (2, 1, 3)], wx_copy, wx_arrived)
    wc_move = Transfer([0] + [d + NX * e for e in parts for d in (1, 3, 2)], wc_copy, wc_arrived)
    wy_move = Transfer((2, 1, 3), wy_copy, wy_arrived)
    wd_move = Transfer((1, 3, 2), wd_copy, wd_arrived)

    def send_part(e):
        wx_move.start([d + NX * e for d in (2, 1, 3)])

    send_part(0)
    pt_move.wait((0,))
    pt_all[xi] = pt_own[...] + pt_sib[...]
    ps_move.wait((0,))
    for a in range(NX):
        ps_stage[core, a] = ps_stage[core, a] + ps_sib[a]
    pt_move.start((2, 1, 3))
    ps_move.start((2, 1, 3))
    wc_move.start((0,))
    send_part(1)
    pt_move.wait((2, 1, 3))
    ps_move.wait((2, 1, 3))
    pt[...] = jnp.sum(pt_all[...], axis=0)
    total = ps_stage[core, xi]
    for d in range(1, NX):
        total = total + ps_recv[d]
    own_half = pl.ds(pl.multiple_of(core * HALF, HALF), HALF)
    pe1_chunks[w] = total / pt[:, own_half]

    def pe_copy(d):
        return to_week(pe1_chunks.at[w], pe1_chunks.at[w], pe_s.at[d], pe_r.at[d], x_peer(d))

    def pe_arrived(d):
        return to_week(pe1_chunks.at[w], pe1_chunks.at[x_from(d)], pe_s.at[d], pe_r.at[d], x_peer(d))

    def pf_copy(d):
        slot = x_from(d)
        return to_week(pe1_chunks.at[slot], pe1_chunks.at[slot], pf_s.at[d], pf_r.at[d], sib)

    def pf_arrived(d):
        slot = other_core(x_from(d))
        return to_week(pe1_chunks.at[slot], pe1_chunks.at[slot], pf_s.at[d], pf_r.at[d], sib)

    pe_move = Transfer((2, 1, 3), pe_copy, pe_arrived)
    pf_move = Transfer((0, 1, 3, 2), pf_copy, pf_arrived)
    pe_move.start()
    pf_move.start((0,))
    for e in parts[2:]:
        send_part(e)

    def wb_half(slot, h):
        return wb.at[
            pl.ds(pl.multiple_of(slot * WK, WK), WK),
            pl.ds(pl.multiple_of(h * HALF, HALF), HALF),
        ]

    for e in parts[:2]:
        for d in (1, 3, 2):
            wx_move.wait((d + NX * e,))
            wc_move.start((d + NX * e,))

    for d in (1, 3, 2):
        pe_move.wait((d,))
        pf_move.start((d,))
    pf_move.wait()
    for r in range(NW):
        pe1[(r // 2) * 8:(r // 2) * 8 + 8, (r % 2) * HALF:(r % 2 + 1) * HALF] = pe1_chunks[r]
    hi, mid, lo = split3(pe1[...])
    pe_rows = jnp.concatenate([hi, mid, lo, jnp.zeros((K, PD), BF16)], axis=0)
    own_wb = wb[pl.ds(pl.multiple_of(w * WK, WK), WK), :]
    taken = lax.dot_general(own_wb, pe_rows, NT, preferred_element_type=F32)
    taken = taken + (pltpu.roll(taken, 128 - K, 1) + pltpu.roll(taken, 128 - 2 * K, 1))
    bt = jnp.where(lane < K, ws - taken, 0.0)
    packed = sum(
        [pltpu.roll(bt[16 * a:16 * a + 16], 32 * a, 1) for a in range(1, 4)], bt[:16]
    )
    b_pack[0] = jnp.concatenate([packed, jnp.broadcast_to(wt_local, (8, 128))], axis=0)

    def by_copy(d):
        return to_prod(b_pack.at[0], b_y.at[d], by_s.at[d], by_r.at[d], grid_peer(8 * d, 1))

    def bz_copy(d):
        return to_prod(b_pack.at[1], b_z.at[d], bz_s.at[d], bz_r.at[d], grid_peer(d, 1))

    by_move = Transfer((2, 1, 3), by_copy)
    bz_move = Transfer((4, 3, 5, 2, 6, 1, 7), bz_copy)
    by_move.start()

    for e in parts[2:]:
        for d in (1, 3, 2):
            wx_move.wait((d + NX * e,))
            wc_move.start((d + NX * e,))
    wy_move.start()
    by_move.wait()
    b_pack[1] = (b_pack[0] + b_y[1]) + (b_y[2] + b_y[3])
    bz_move.start()
    hi, mid, lo = split3(wfull[w] / pt[...])
    wc_move.wait()

    for h in (0, 1):
        wb_half(sib, h)[...] = half_of(sib, h)[...].astype(BF16)

    def to_bf16(i):
        d = 1 + i // 2
        slot = chip_from(d) * 2 + lax.rem(i, 2)
        h = first_half(xi, chip_from(d))
        wb_half(slot, h)[...] = half_of(slot, h)[...].astype(BF16)
        wb_half(slot, 1 - h)[...] = jnp.zeros((WK, HALF), BF16)

    loop(0, NW - 2, to_bf16)
    rows = jnp.concatenate([hi, mid, lo], axis=0)
    m3 = lax.dot_general(rows, wb[...], NT, preferred_element_type=F32)
    m_own = m3[:WK] + (m3[WK:2 * WK] + m3[2 * WK:])
    for q in range(NP):
        m_stage[q] = m_own[(q // 4) * 8:(q // 4) * 8 + 8, (q % 4) * 128:(q % 4 + 1) * 128]

    def ms_copy(d):
        q = prod_peer(d)
        return to_prod(m_stage.at[q], m_recv.at[d], ms_s.at[d], ms_r.at[d], q)

    ms_move = Transfer(range(1, NP), ms_copy)
    pl.semaphore_wait(ready, 7)
    ms_move.start()

    bz_move.wait()
    packed = sum([b_z[d] for d in range(1, 8)], b_pack[1])
    wt_own = jnp.sum(jnp.where(lane == row, packed[16:17], 0.0), axis=1, keepdims=True)
    packed = packed[:16]
    b_own = jnp.concatenate(
        [packed] + [pltpu.roll(packed, 128 - 32 * a, 1) for a in range(1, 4)], axis=0
    )
    b_own = jnp.where(lane < K, b_own, jnp.where(lane == K, wt_own, 0.0))
    b_all[w] = b_own[:32] + pltpu.roll(b_own[32:], 64, 1)
    own_rows = pl.ds(pl.multiple_of(w * WK, WK), WK)

    def ba_copy(d):
        return to_week(b_all.at[w], b_all.at[w], ba_s.at[d], ba_r.at[d], week_peer(d))

    def ba_arrived(d):
        return to_week(b_all.at[w], b_all.at[lax.rem(w + NW - d, NW)], ba_s.at[d], ba_r.at[d], week_peer(d))

    ba_move = Transfer(range(1, NW), ba_copy, ba_arrived)
    ba_move.start()

    we_buf[pl.ds(0, WK), :] = b_own / wt_own

    def r_pair(j):
        we1 = we_buf[pl.ds(0, WK), :]
        cols = [
            jnp.sum(jnp.where(lane == 2 * j + e, we1, 0.0), axis=1, keepdims=True)
            for e in range(2)
        ]
        at = pl.ds(pl.multiple_of(j * 16, 16), 16)
        for c in range(PD // 256):
            lanes = slice(c * 256, (c + 1) * 256)
            cellw = wfull[w, :, lanes]
            fs = []
            for e in range(2):
                k = 2 * j + e
                f = x[k, :, lanes].astype(F32) - pe1[pl.ds(k, 1), lanes] - cols[e]
                fs.append(f)
            for g in range(8):
                s = slice(g * 8, g * 8 + 8)
                pair = jnp.concatenate([fs[0][s], fs[1][s]], axis=0)
                wpair = jnp.concatenate([fs[0][s] * cellw[s], fs[1][s] * cellw[s]], axis=0)
                q_buf[g, at, lanes] = pair.astype(BF16)
                u_buf[g, at, lanes] = wpair.astype(BF16)

    loop(0, R_FIRST, r_pair)

    ms_move.wait()
    tile = lax.fori_loop(1, NP, lambda d, a: a + m_recv[d], m_stage[p])

    def tile_of(wk, q):
        return mm.at[
            pl.ds(pl.multiple_of(wk * WK + (q // 4) * 8, 8), 8),
            pl.ds(pl.multiple_of(lax.rem(q, 4) * 128, 128), 128),
        ]

    tile_of(w, p)[...] = tile

    def ma_copy(d):
        return to_prod(tile_of(w, p), tile_of(w, p), ma_s.at[d], ma_r.at[d], grid_peer(d, 1))

    def ma_arrived(d):
        return to_prod(tile_of(w, p), tile_of(w, grid_peer(d, -1)), ma_s.at[d], ma_r.at[d], grid_peer(d, 1))

    def forward_tile(q):
        for d in (2, 1, 3):
            to_week(tile_of(w, q), tile_of(w, q), mx_s.at[d], mx_r.at[d], x_peer(d)).start()

    near_first = sorted(
        range(1, NP), key=lambda d: min(d // 8, 4 - d // 8) + min(d % 8, 8 - d % 8)
    )
    ma_move = Transfer(near_first, ma_copy, ma_arrived)
    ma_move.start(near_first[::-1])
    forward_tile(p)

    for d in (1, 3, 2):
        wy_move.wait((d,))
        wd_move.start((d,))

    def r_dot(g, acc):
        return acc + lax.dot_general(u_buf[g], q_buf[g], NT, preferred_element_type=F32)

    def forward_tiles(ds):
        for d in ds:
            ma_move.wait((d,))
            forward_tile(grid_peer(d, -1))

    loop(R_FIRST, K // 2, r_pair)
    big = lax.fori_loop(0, 5, r_dot, jnp.zeros((K * 8, K * 8), F32))
    forward_tiles(near_first[:6])
    big = lax.fori_loop(5, 7, r_dot, big)
    forward_tiles(near_first[6:14])
    big = r_dot(7, big)
    ri = lax.broadcasted_iota(jnp.int32, (K * 8, K * 8), 0)
    ci = lax.broadcasted_iota(jnp.int32, (K * 8, K * 8), 1)
    big = jnp.where(lax.rem(ri, 8) == lax.rem(ci, 8), big, 0.0)
    ei = lax.broadcasted_iota(jnp.int32, (K, K * 8), 0)
    ej = lax.broadcasted_iota(jnp.int32, (K, K * 8), 1)
    fold = jnp.where(ei == ej // 8, 1.0, 0.0)
    fi = lax.broadcasted_iota(jnp.int32, (K * 8, 128), 0)
    fj = lax.broadcasted_iota(jnp.int32, (K * 8, 128), 1)
    fold_t = jnp.where(fi // 8 == fj, 1.0, 0.0)
    half_done = lax.dot_general(fold, big, NN, precision=HI, preferred_element_type=F32)
    r2 = lax.dot_general(half_done, fold_t, NN, precision=HI, preferred_element_type=F32)
    r_pack[0] = r2[0:8] + pltpu.roll(r2[8:16], 32, 1) + pltpu.roll(r2[16:24], 64, 1) + pltpu.roll(r2[24:32], 96, 1)

    def rw_copy(d):
        return to_week(r_pack.at[0], r_week.at[d], rw_s.at[d], rw_r.at[d], week_peer(d))

    rw_move = Transfer(range(1, NW), rw_copy)
    rw_move.start()

    forward_tiles(near_first[14:])

    def rows_of(wk):
        return mm.at[pl.ds(pl.multiple_of(wk * WK, WK), WK)]

    def mx_copy(d):
        return to_week(rows_of(w), rows_of(w), mx_s.at[d], mx_r.at[d], x_peer(d))

    def mx_arrived(d):
        return to_week(rows_of(w), rows_of(x_from(d)), mx_s.at[d], mx_r.at[d], x_peer(d))

    def mc_copy(d):
        slot = x_from(d)
        return to_week(rows_of(slot), rows_of(slot), mc_s.at[d], mc_r.at[d], sib)

    def mc_arrived(d):
        slot = x_from(d) + 1 - 2 * core
        return to_week(rows_of(slot), rows_of(slot), mc_s.at[d], mc_r.at[d], sib)

    mx_move = Transfer((1, 3, 2), mx_copy, mx_arrived)
    mc_move = Transfer((0, 1, 3, 2), mc_copy, mc_arrived)
    mx_move.sent += [1, 3, 2]
    mc_move.start((0,))

    rw_move.wait()
    r_sum = r_pack[0]
    for d in range(1, NW):
        r_sum = r_sum + r_week[d]
    r_pack[1] = r_sum

    def rp_copy(d):
        return to_prod(r_pack.at[1], r_prod.at[d], rp_s.at[d], rp_r.at[d], prod_peer(d))

    rp_move = Transfer(range(1, NP), rp_copy)
    rp_move.start()
    for d in (1, 3, 2):
        mx_move.wait((d,))
        mc_move.start((d,))
    wd_move.wait()

    def rest_to_bf16(i):
        d = 1 + i // 2
        slot = chip_from(d) * 2 + lax.rem(i, 2)
        h = 1 - first_half(xi, chip_from(d))
        wb_half(slot, h)[...] = half_of(slot, h)[...].astype(BF16)

    loop(0, NW - 2, rest_to_bf16)

    ba_move.wait()
    lane_all = lax.broadcasted_iota(jnp.int32, (WEEKS, 128), 1)
    pieces = []
    for i in range(NW):
        piece = b_all[i]
        pieces += [piece, pltpu.roll(piece, 64, 1)]
    b = jnp.concatenate(pieces, axis=0)
    wt = jnp.sum(jnp.where(lane_all == K, b, 0.0), axis=1, keepdims=True)
    b = jnp.where(lane_all < K, b, 0.0)
    we1 = b / wt
    weight_total = jnp.sum(wt, axis=0, keepdims=True)

    mc_move.wait()

    def put_m(rows, cols, v):
        hi, mid, lo = split3(v)
        m_hi[rows, cols] = hi
        m_mid[rows, cols] = mid
        m_lo[rows, cols] = lo

    blocks = [slice(a * 128, a * 128 + 128) for a in range(NX)]
    for a in range(NX):
        put_m(blocks[a], blocks[a], mm[blocks[a], blocks[a]])
        for c in range(a + 1, NX):
            both = mm[blocks[a], blocks[c]] + mm[blocks[c], blocks[a]].T
            put_m(blocks[a], blocks[c], both)
            put_m(blocks[c], blocks[a], both.T)

    def apply_m(v):
        hi, mid, lo = [part.astype(F32) for part in split3(v)]
        parts = (hi + pltpu.roll(mid, K, 1) + pltpu.roll(lo, 2 * K, 1)).astype(BF16)
        acc = jnp.dot(m_hi[...], parts, preferred_element_type=F32)
        acc = acc + jnp.where(lane_all < 2 * K, jnp.dot(m_mid[...], parts, preferred_element_type=F32), 0.0)
        acc = acc + jnp.where(lane_all < K, jnp.dot(m_lo[...], parts, preferred_element_type=F32), 0.0)
        acc = acc + (pltpu.roll(acc, 128 - K, 1) + pltpu.roll(acc, 128 - 2 * K, 1))
        return jnp.where(lane_all < K, acc, 0.0)

    n1 = apply_m(we1)
    we2 = (b + n1) / wt
    we3 = (b + apply_m(we2)) / wt
    n3 = apply_m(we3)
    we4 = (b + n3) / wt
    we_buf[...] = we4
    we4_out[...] = we_buf[own_rows, :]

    we3_t = we3.T[:K]
    hi, mid, lo = split3(we3_t)
    rows = jnp.concatenate([hi, mid, lo], axis=0)
    wp3 = lax.dot_general(rows, wb[...], NN, preferred_element_type=F32)
    wp = wp3[:K] + (wp3[K:2 * K] + wp3[2 * K:])
    pe4_out[...] = pe1[...] - wp / pt[...]

    rp_move.wait()
    r_total = lax.fori_loop(1, NP, lambda d, a: a + r_prod[d], r_pack[1])
    gram = lax.dot_general((we3 - we4).T[:K], n3, NN, precision=HI, preferred_element_type=F32)
    gram = gram - lax.dot_general(we3_t, n1, NN, precision=HI, preferred_element_type=F32)
    r_rows = jnp.concatenate(
        [r_total] + [pltpu.roll(r_total, 128 - 32 * a, 1) for a in range(1, 4)], axis=0
    )
    gram_out[...] = ((r_rows + gram) / weight_total)[:, :K]

    for move in (
        pt_move, ps_move, wx_move, wc_move, wy_move, wd_move, pe_move, pf_move, by_move, bz_move, ba_move,
        ms_move, ma_move, mx_move, mc_move, rw_move, rp_move,
    ):
        move.drain()


def effects(x, cell):
    vmem = pl.BlockSpec(memory_space=pltpu.VMEM)
    dma = pltpu.SemaphoreType.DMA
    scratch = [
        pltpu.VMEM((K, WK, PD), BF16),
        pltpu.VMEM((NW, WK, PD), F32),
        pltpu.VMEM((WEEKS, PD), BF16),
        pltpu.VMEM((1, PD), F32),
        pltpu.VMEM((1, PD), F32),
        pltpu.VMEM((NX, 1, PD), F32),
        pltpu.VMEM((1, PD), F32),
        pltpu.VMEM((2, NX, 8, HALF), F32),
        pltpu.VMEM((NX, 8, HALF), F32),
        pltpu.VMEM((NX, 8, HALF), F32),
        pltpu.VMEM((NW, 8, HALF), F32),
        pltpu.VMEM((K, PD), F32),
        pltpu.VMEM((2, 24, 128), F32),
        pltpu.VMEM((4, 24, 128), F32),
        pltpu.VMEM((8, 24, 128), F32),
        pltpu.VMEM((NW, 32, 128), F32),
        pltpu.VMEM((NP, 8, 128), F32),
        pltpu.VMEM((NP, 8, 128), F32),
        pltpu.VMEM((WEEKS, WEEKS), F32),
        pltpu.VMEM((WEEKS, WEEKS), BF16),
        pltpu.VMEM((WEEKS, WEEKS), BF16),
        pltpu.VMEM((WEEKS, WEEKS), BF16),
        pltpu.VMEM((8, K * 8, PD), BF16),
        pltpu.VMEM((8, K * 8, PD), BF16),
        pltpu.VMEM((2, 8, 128), F32),
        pltpu.VMEM((NW, 8, 128), F32),
        pltpu.VMEM((NP, 8, 128), F32),
        pltpu.VMEM((WEEKS, 128), F32),
        dma((4,)),
        pltpu.SemaphoreType.REGULAR,
    ]
    for n in (NX, NX, NX, NX, len(W_PARTS) * NX, len(W_PARTS) * NX, NX, NX, 4, 8, NW, NP, NP, NX, NX, NW, NP):
        scratch += [dma((n,)), dma((n,))]
    return pl.pallas_call(
        effects_kernel,
        out_shape=(
            jax.ShapeDtypeStruct((K, PD), F32),
            jax.ShapeDtypeStruct((WK, 128), F32),
            jax.ShapeDtypeStruct((K, K), F32),
        ),
        in_specs=[pl.BlockSpec(memory_space=pl.ANY), vmem],
        out_specs=(vmem, vmem, vmem),
        scratch_shapes=scratch,
        compiler_params=pltpu.CompilerParams(
            collective_id=0, has_side_effects=True, vmem_limit_bytes=VMEM_LIMIT
        ),
        name="effects",
    )(x, cell)


KB = 4


def output_kernel(x, cell, pe4, we4, gram, out_hbm, gram_out, out, sem):
    gram_out[...] = gram[...]
    lane = lax.broadcasted_iota(jnp.int32, (WK, 128), 1)

    def copy(i):
        rows = pl.ds(i * KB, KB)
        return pltpu.make_async_copy(out.at[rows], out_hbm.at[rows], sem.at[i])

    def block(i):
        for e in range(KB):
            k = i * KB + e
            col = jnp.sum(jnp.where(lane == k, we4[...], 0.0), axis=1, keepdims=True)
            for c in range(PD // LC):
                lanes = slice(c * LC, (c + 1) * LC)
                field = x[k, :, lanes].astype(F32) - pe4[pl.ds(k, 1), lanes] - col
                out[k, :, lanes] = jnp.where(cell[:, lanes] > 0.0, field, 0.0).astype(BF16)
        copy(i).start()

    loop(0, K // KB, block)
    loop(0, K // KB, lambda i: copy(i).wait())


def output(x, cell, pe4, we4, gram):
    vmem = pl.BlockSpec(memory_space=pltpu.VMEM)
    return pl.pallas_call(
        output_kernel,
        out_shape=(
            jax.ShapeDtypeStruct((K, WK, PD), BF16),
            jax.ShapeDtypeStruct((K, K), F32),
        ),
        in_specs=[vmem] * 5,
        out_specs=(pl.BlockSpec(memory_space=pl.ANY), vmem),
        scratch_shapes=[pltpu.VMEM((K, WK, PD), BF16), pltpu.SemaphoreType.DMA((K // KB,))],
        compiler_params=pltpu.CompilerParams(vmem_limit_bytes=32 * 2**20),
        name="output",
    )(x, cell, pe4, we4, gram)


def per_device(regressors, weights, first_week, last_week):
    ids = lax.axis_index("week") * WK + lax.broadcasted_iota(jnp.int32, (WK, PD), 0)
    live = (ids >= first_week[None, :]) & (ids <= last_week[None, :])
    cell = jnp.where(live, weights.astype(F32), 0.0)
    pe4, we4, gram = effects(regressors, cell)
    return output(regressors, cell, pe4, we4, gram)


def solution(mesh):
    return jax.shard_map(
        per_device,
        mesh=mesh,
        in_specs=(P(None, "week", "prod"), P("week", "prod"), P("prod"), P("prod")),
        out_specs=(P(None, "week", "prod"), P()),
        check_vma=False,
    )
```

```python
import functools

import jax
import jax.numpy as jnp
from jax import lax
from jax.experimental import pallas as pl
from jax.experimental.pallas import tpu as pltpu
from jax.sharding import PartitionSpec as P

MESH = pl.DeviceIdType.MESH
F32 = jnp.float32
BF16 = jnp.bfloat16
HI = lax.Precision.HIGHEST
NT = (((1,), (1,)), ((), ()))
NN = (((1,), (0,)), ((), ()))

K = 32
WK = 64
PD = 1536
NW = 8
NX = 4
NP = 32
WEEKS = NW * WK
LC = 384
HALF = PD // 2
W_PARTS = (0, 8, 40, 64)
R_FIRST = 10
VMEM_LIMIT = 53 * 2**20


def split3(v):
    hi = v.astype(BF16)
    r = v - hi.astype(F32)
    mid = r.astype(BF16)
    lo = (r - mid.astype(F32)).astype(BF16)
    return hi, mid, lo


def loop(lo, hi, body):
    def step(i, carry):
        body(i)
        return carry

    lax.fori_loop(lo, hi, step, 0)


class Transfer:
    def __init__(self, ds, send, arrival=None):
        self.ds, self.send, self.arrival = ds, send, arrival or send
        self.sent, self.got = [], []

    def each(self, ds, act):
        if isinstance(ds, range) and len(ds) > 3:
            loop(ds.start, ds.stop, act)
        else:
            for d in ds:
                act(d)

    def start(self, ds=None):
        ds = self.ds if ds is None else ds
        self.each(ds, lambda d: self.send(d).start())
        self.sent += list(ds)

    def wait(self, ds=None):
        ds = self.ds if ds is None else ds
        self.each(ds, lambda d: self.arrival(d).wait_recv())
        self.got += list(ds)

    def drain(self):
        self.each(self.ds if len(self.sent) == len(self.ds) else self.sent, lambda d: self.send(d).wait_send())


def effects_kernel(
    x_hbm, cell_in,
    pe4_out, we4_out, gram_out,
    x, wfull, wb, pt_own, pt_sib, pt_all, pt, ps_stage, ps_sib, ps_recv, pe1_chunks, pe1,
    b_pack, b_y, b_z, b_all, m_stage, m_recv, mm, m_hi, m_mid, m_lo,
    q_buf, u_buf, r_pack, r_week, r_prod, we_buf,
    x_sem, ready, pt_s, pt_r, ps_s, ps_r, pe_s, pe_r, pf_s, pf_r, wx_s, wx_r, wc_s, wc_r, wy_s, wy_r, wd_s, wd_r,
    by_s, by_r, bz_s, bz_r, ba_s, ba_r, ms_s, ms_r, ma_s, ma_r, mx_s, mx_r, mc_s, mc_r,
    rw_s, rw_r, rp_s, rp_r,
):
    w = lax.axis_index("week")
    p = lax.axis_index("prod")
    xi = w // 2
    core = lax.rem(w, 2)
    sib = xi * 2 + (1 - core)

    def week_peer(d):
        return lax.rem(w + d, NW)

    def prod_peer(d):
        return lax.rem(p + d, NP)

    def grid_peer(d, sign):
        y = lax.rem(p // 8 + 4 + sign * (d // 8), 4)
        z = lax.rem(lax.rem(p, 8) + 8 + sign * (d % 8), 8)
        return y * 8 + z

    def x_peer(d):
        return lax.rem(xi + d, NX) * 2 + core

    def x_from(d):
        return lax.rem(xi + NX - d, NX) * 2 + core

    def to_week(src, dst, ssem, rsem, q):
        return pltpu.make_async_remote_copy(
            src_ref=src, dst_ref=dst, send_sem=ssem, recv_sem=rsem,
            device_id={"week": q}, device_id_type=MESH,
        )

    def to_prod(src, dst, ssem, rsem, q):
        return pltpu.make_async_remote_copy(
            src_ref=src, dst_ref=dst, send_sem=ssem, recv_sem=rsem,
            device_id={"prod": q}, device_id_type=MESH,
        )

    def x_copy(c):
        rows = pl.ds(c * 8, 8)
        return pltpu.make_async_copy(x_hbm.at[rows], x.at[rows], x_sem.at[c])

    for c in range(4):
        x_copy(c).start()

    barrier = pltpu.get_barrier_semaphore()

    def greet_week(d):
        pl.semaphore_signal(barrier, inc=1, device_id={"week": week_peer(d)}, device_id_type=MESH)

    def greet_grid(d):
        pl.semaphore_signal(barrier, inc=1, device_id={"prod": grid_peer(d, 1)}, device_id_type=MESH)

    loop(1, NW, greet_week)
    loop(1, 4, lambda d: greet_grid(8 * d))
    loop(1, 8, greet_grid)

    cell = cell_in[...]
    wfull[w] = cell
    wb[pl.ds(pl.multiple_of(w * WK, WK), WK), :] = cell.astype(BF16)
    pt_own[...] = jnp.sum(cell, axis=0, keepdims=True)
    lane = lax.broadcasted_iota(jnp.int32, (WK, 128), 1)
    row = lax.broadcasted_iota(jnp.int32, (WK, 128), 0)
    wt_col = jnp.sum(cell, axis=1, keepdims=True)
    wt_local = jnp.sum(jnp.where(lane == row, wt_col, 0.0), axis=0, keepdims=True)

    def sums_group(g, acc):
        x_copy(g).wait()

        def one(j, acc):
            k = g * 8 + j
            part = jnp.zeros((WK, 128), F32)
            for c in range(PD // LC):
                lanes = slice(c * LC, (c + 1) * LC)
                weighted = x[k, :, lanes].astype(F32) * wfull[w, :, lanes]
                half, off = c // 2, (c % 2) * LC
                ps_stage[half, g, pl.ds(j, 1), off:off + LC] = jnp.sum(weighted, axis=0, keepdims=True)
                for t in range(LC // 128):
                    part = part + weighted[:, t * 128:(t + 1) * 128]
            return acc + jnp.where(lane == k, jnp.sum(part, axis=1, keepdims=True), 0.0)

        return lax.fori_loop(0, 8, one, acc, unroll=8)

    ws = lax.fori_loop(0, 3, sums_group, jnp.zeros((WK, 128), F32))

    pl.semaphore_wait(barrier, NW - 1 + 3 + 7)

    def pass_on(d):
        pl.semaphore_signal(ready, inc=1, device_id={"prod": grid_peer(d, 1)}, device_id_type=MESH)

    loop(1, 8, pass_on)

    def pt_copy(d):
        if d == 0:
            return to_week(pt_own, pt_sib, pt_s.at[0], pt_r.at[0], sib)
        return to_week(pt_all.at[xi], pt_all.at[xi], pt_s.at[d], pt_r.at[d], x_peer(d))

    def pt_arrived(d):
        if d == 0:
            return pt_copy(0)
        return to_week(pt_all.at[xi], pt_all.at[lax.rem(xi + NX - d, NX)], pt_s.at[d], pt_r.at[d], x_peer(d))

    def ps_copy(d):
        if d == 0:
            return to_week(ps_stage.at[1 - core], ps_sib, ps_s.at[0], ps_r.at[0], sib)
        q = x_peer(d)
        return to_week(ps_stage.at[core, lax.rem(xi + d, NX)], ps_recv.at[d], ps_s.at[d], ps_r.at[d], q)

    pt_move = Transfer((0, 2, 1, 3), pt_copy, pt_arrived)
    ps_move = Transfer((0, 2, 1, 3), ps_copy)
    pt_move.start((0,))

    def first_half(chip, other):
        return jnp.where(chip < other, 0, 1)

    def half_of(slot, h):
        return wfull.at[slot, :, pl.ds(pl.multiple_of(h * HALF, HALF), HALF)]

    def chip_to(d):
        return lax.rem(xi + d, NX)

    def chip_from(d):
        return lax.rem(xi + NX - d, NX)

    def part_of(slot, h, e):
        lo, hi = W_PARTS[e], W_PARTS[e + 1]
        return wfull.at[slot, pl.ds(lo, hi - lo), pl.ds(pl.multiple_of(h * HALF, HALF), HALF)]

    def wx_copy(i):
        d, e = i % NX, i // NX
        h = first_half(chip_to(d), xi)
        return to_week(part_of(w, h, e), part_of(w, h, e), wx_s.at[i], wx_r.at[i], x_peer(d))

    def wx_arrived(i):
        d, e = i % NX, i // NX
        h = first_half(xi, chip_from(d))
        return to_week(part_of(w, h, e), part_of(x_from(d), h, e), wx_s.at[i], wx_r.at[i], x_peer(d))

    def wy_copy(d):
        h = 1 - first_half(chip_to(d), xi)
        return to_week(half_of(w, h), half_of(w, h), wy_s.at[d], wy_r.at[d], x_peer(d))

    def wy_arrived(d):
        h = 1 - first_half(xi, chip_from(d))
        return to_week(half_of(w, h), half_of(x_from(d), h), wy_s.at[d], wy_r.at[d], x_peer(d))

    def other_core(slot):
        return slot + 1 - 2 * core

    def wc_copy(i):
        d, e = i % NX, i // NX
        if d == 0:
            return to_week(wfull.at[w], wfull.at[w], wc_s.at[i], wc_r.at[i], sib)
        here = part_of(x_from(d), first_half(xi, chip_from(d)), e)
        return to_week(here, here, wc_s.at[i], wc_r.at[i], sib)

    def wc_arrived(i):
        d, e = i % NX, i // NX
        if d == 0:
            return to_week(wfull.at[w], wfull.at[sib], wc_s.at[i], wc_r.at[i], sib)
        here = part_of(other_core(x_from(d)), first_half(xi, chip_from(d)), e)
        return to_week(here, here, wc_s.at[i], wc_r.at[i], sib)

    def wd_copy(d):
        here = half_of(x_from(d), 1 - first_half(xi, chip_from(d)))
        return to_week(here, here, wd_s.at[d], wd_r.at[d], sib)

    def wd_arrived(d):
        here = half_of(other_core(x_from(d)), 1 - first_half(xi, chip_from(d)))
        return to_week(here, here, wd_s.at[d], wd_r.at[d], sib)

    parts = range(len(W_PARTS) - 1)
    wx_move = Transfer([d + NX * e for e in parts for d in (2, 1, 3)], wx_copy, wx_arrived)
    wc_move = Transfer([0] + [d + NX * e for e in parts for d in (1, 3, 2)], wc_copy, wc_arrived)
    wy_move = Transfer((2, 1, 3), wy_copy, wy_arrived)
    wd_move = Transfer((1, 3, 2), wd_copy, wd_arrived)

    def send_part(e):
        wx_move.start([d + NX * e for d in (2, 1, 3)])

    send_part(0)
    ws = lax.fori_loop(3, 4, sums_group, ws)
    ps_move.start((0,))
    pt_move.wait((0,))
    pt_all[xi] = pt_own[...] + pt_sib[...]
    ps_move.wait((0,))
    for a in range(NX):
        ps_stage[core, a] = ps_stage[core, a] + ps_sib[a]
    pt_move.start((2, 1, 3))
    ps_move.start((2, 1, 3))
    wc_move.start((0,))
    send_part(1)
    pt_move.wait((2, 1, 3))
    ps_move.wait((2, 1, 3))
    pt[...] = jnp.sum(pt_all[...], axis=0)
    total = ps_stage[core, xi]
    for d in range(1, NX):
        total = total + ps_recv[d]
    own_half = pl.ds(pl.multiple_of(core * HALF, HALF), HALF)
    pe1_chunks[w] = total / pt[:, own_half]

    def pe_copy(d):
        return to_week(pe1_chunks.at[w], pe1_chunks.at[w], pe_s.at[d], pe_r.at[d], x_peer(d))

    def pe_arrived(d):
        return to_week(pe1_chunks.at[w], pe1_chunks.at[x_from(d)], pe_s.at[d], pe_r.at[d], x_peer(d))

    def pf_copy(d):
        slot = x_from(d)
        return to_week(pe1_chunks.at[slot], pe1_chunks.at[slot], pf_s.at[d], pf_r.at[d], sib)

    def pf_arrived(d):
        slot = other_core(x_from(d))
        return to_week(pe1_chunks.at[slot], pe1_chunks.at[slot], pf_s.at[d], pf_r.at[d], sib)

    pe_move = Transfer((2, 1, 3), pe_copy, pe_arrived)
    pf_move = Transfer((0, 1, 3, 2), pf_copy, pf_arrived)
    pe_move.start()
    pf_move.start((0,))
    for e in parts[2:]:
        send_part(e)

    def wb_half(slot, h):
        return wb.at[
            pl.ds(pl.multiple_of(slot * WK, WK), WK),
            pl.ds(pl.multiple_of(h * HALF, HALF), HALF),
        ]

    for e in parts[:2]:
        for d in (1, 3, 2):
            wx_move.wait((d + NX * e,))
            wc_move.start((d + NX * e,))

    for d in (1, 3, 2):
        pe_move.wait((d,))
        pf_move.start((d,))
    pf_move.wait()
    for r in range(NW):
        pe1[(r // 2) * 8:(r // 2) * 8 + 8, (r % 2) * HALF:(r % 2 + 1) * HALF] = pe1_chunks[r]
    hi, mid, lo = split3(pe1[...])
    pe_rows = jnp.concatenate([hi, mid, lo, jnp.zeros((K, PD), BF16)], axis=0)
    own_wb = wb[pl.ds(pl.multiple_of(w * WK, WK), WK), :]
    taken = lax.dot_general(own_wb, pe_rows, NT, preferred_element_type=F32)
    taken = taken + (pltpu.roll(taken, 128 - K, 1) + pltpu.roll(taken, 128 - 2 * K, 1))
    bt = jnp.where(lane < K, ws - taken, 0.0)
    packed = sum(
        [pltpu.roll(bt[16 * a:16 * a + 16], 32 * a, 1) for a in range(1, 4)], bt[:16]
    )
    b_pack[0] = jnp.concatenate([packed, jnp.broadcast_to(wt_local, (8, 128))], axis=0)

    def by_copy(d):
        return to_prod(b_pack.at[0], b_y.at[d], by_s.at[d], by_r.at[d], grid_peer(8 * d, 1))

    def bz_copy(d):
        return to_prod(b_pack.at[1], b_z.at[d], bz_s.at[d], bz_r.at[d], grid_peer(d, 1))

    by_move = Transfer((2, 1, 3), by_copy)
    bz_move = Transfer((4, 3, 5, 2, 6, 1, 7), bz_copy)
    by_move.start()

    for e in parts[2:]:
        for d in (1, 3, 2):
            wx_move.wait((d + NX * e,))
            wc_move.start((d + NX * e,))
    wy_move.start()
    by_move.wait()
    b_pack[1] = (b_pack[0] + b_y[1]) + (b_y[2] + b_y[3])
    bz_move.start()
    hi, mid, lo = split3(wfull[w] / pt[...])
    wc_move.wait()

    for h in (0, 1):
        wb_half(sib, h)[...] = half_of(sib, h)[...].astype(BF16)

    def to_bf16(i):
        d = 1 + i // 2
        slot = chip_from(d) * 2 + lax.rem(i, 2)
        h = first_half(xi, chip_from(d))
        wb_half(slot, h)[...] = half_of(slot, h)[...].astype(BF16)
        wb_half(slot, 1 - h)[...] = jnp.zeros((WK, HALF), BF16)

    loop(0, NW - 2, to_bf16)
    rows = jnp.concatenate([hi, mid, lo], axis=0)
    m3 = lax.dot_general(rows, wb[...], NT, preferred_element_type=F32)
    m_own = m3[:WK] + (m3[WK:2 * WK] + m3[2 * WK:])
    for q in range(NP):
        m_stage[q] = m_own[(q // 4) * 8:(q // 4) * 8 + 8, (q % 4) * 128:(q % 4 + 1) * 128]

    def ms_copy(d):
        q = prod_peer(d)
        return to_prod(m_stage.at[q], m_recv.at[d], ms_s.at[d], ms_r.at[d], q)

    ms_move = Transfer(range(1, NP), ms_copy)
    pl.semaphore_wait(ready, 7)
    ms_move.start()

    bz_move.wait()
    packed = sum([b_z[d] for d in range(1, 8)], b_pack[1])
    wt_own = jnp.sum(jnp.where(lane == row, packed[16:17], 0.0), axis=1, keepdims=True)
    packed = packed[:16]
    b_own = jnp.concatenate(
        [packed] + [pltpu.roll(packed, 128 - 32 * a, 1) for a in range(1, 4)], axis=0
    )
    b_own = jnp.where(lane < K, b_own, jnp.where(lane == K, wt_own, 0.0))
    b_all[w] = b_own[:32] + pltpu.roll(b_own[32:], 64, 1)
    own_rows = pl.ds(pl.multiple_of(w * WK, WK), WK)

    def ba_copy(d):
        return to_week(b_all.at[w], b_all.at[w], ba_s.at[d], ba_r.at[d], week_peer(d))

    def ba_arrived(d):
        return to_week(b_all.at[w], b_all.at[lax.rem(w + NW - d, NW)], ba_s.at[d], ba_r.at[d], week_peer(d))

    ba_move = Transfer(range(1, NW), ba_copy, ba_arrived)
    ba_move.start()

    we_buf[pl.ds(0, WK), :] = b_own / wt_own

    def r_pair(j):
        we1 = we_buf[pl.ds(0, WK), :]
        cols = [
            jnp.sum(jnp.where(lane == 2 * j + e, we1, 0.0), axis=1, keepdims=True)
            for e in range(2)
        ]
        at = pl.ds(pl.multiple_of(j * 16, 16), 16)
        for c in range(PD // 256):
            lanes = slice(c * 256, (c + 1) * 256)
            cellw = wfull[w, :, lanes]
            fs = []
            for e in range(2):
                k = 2 * j + e
                f = x[k, :, lanes].astype(F32) - pe1[pl.ds(k, 1), lanes] - cols[e]
                fs.append(f)
            for g in range(8):
                s = slice(g * 8, g * 8 + 8)
                pair = jnp.concatenate([fs[0][s], fs[1][s]], axis=0)
                wpair = jnp.concatenate([fs[0][s] * cellw[s], fs[1][s] * cellw[s]], axis=0)
                q_buf[g, at, lanes] = pair.astype(BF16)
                u_buf[g, at, lanes] = wpair.astype(BF16)

    loop(0, R_FIRST, r_pair)

    ms_move.wait()
    tile = lax.fori_loop(1, NP, lambda d, a: a + m_recv[d], m_stage[p])

    def tile_of(wk, q):
        return mm.at[
            pl.ds(pl.multiple_of(wk * WK + (q // 4) * 8, 8), 8),
            pl.ds(pl.multiple_of(lax.rem(q, 4) * 128, 128), 128),
        ]

    tile_of(w, p)[...] = tile

    def ma_copy(d):
        return to_prod(tile_of(w, p), tile_of(w, p), ma_s.at[d], ma_r.at[d], grid_peer(d, 1))

    def ma_arrived(d):
        return to_prod(tile_of(w, p), tile_of(w, grid_peer(d, -1)), ma_s.at[d], ma_r.at[d], grid_peer(d, 1))

    def forward_tile(q):
        for d in (2, 1, 3):
            to_week(tile_of(w, q), tile_of(w, q), mx_s.at[d], mx_r.at[d], x_peer(d)).start()

    near_first = sorted(
        range(1, NP), key=lambda d: min(d // 8, 4 - d // 8) + min(d % 8, 8 - d % 8)
    )
    ma_move = Transfer(near_first, ma_copy, ma_arrived)
    ma_move.start(near_first[::-1])
    forward_tile(p)

    for d in (1, 3, 2):
        wy_move.wait((d,))
        wd_move.start((d,))

    def r_dot(g, acc):
        return acc + lax.dot_general(u_buf[g], q_buf[g], NT, preferred_element_type=F32)

    def forward_tiles(ds):
        for d in ds:
            ma_move.wait((d,))
            forward_tile(grid_peer(d, -1))

    loop(R_FIRST, K // 2, r_pair)
    big = lax.fori_loop(0, 5, r_dot, jnp.zeros((K * 8, K * 8), F32))
    forward_tiles(near_first[:6])
    big = lax.fori_loop(5, 7, r_dot, big)
    forward_tiles(near_first[6:14])
    big = r_dot(7, big)
    ri = lax.broadcasted_iota(jnp.int32, (K * 8, K * 8), 0)
    ci = lax.broadcasted_iota(jnp.int32, (K * 8, K * 8), 1)
    big = jnp.where(lax.rem(ri, 8) == lax.rem(ci, 8), big, 0.0)
    ei = lax.broadcasted_iota(jnp.int32, (K, K * 8), 0)
    ej = lax.broadcasted_iota(jnp.int32, (K, K * 8), 1)
    fold = jnp.where(ei == ej // 8, 1.0, 0.0)
    fi = lax.broadcasted_iota(jnp.int32, (K * 8, 128), 0)
    fj = lax.broadcasted_iota(jnp.int32, (K * 8, 128), 1)
    fold_t = jnp.where(fi // 8 == fj, 1.0, 0.0)
    half_done = lax.dot_general(fold, big, NN, precision=HI, preferred_element_type=F32)
    r2 = lax.dot_general(half_done, fold_t, NN, precision=HI, preferred_element_type=F32)
    r_pack[0] = r2[0:8] + pltpu.roll(r2[8:16], 32, 1) + pltpu.roll(r2[16:24], 64, 1) + pltpu.roll(r2[24:32], 96, 1)

    def rw_copy(d):
        return to_week(r_pack.at[0], r_week.at[d], rw_s.at[d], rw_r.at[d], week_peer(d))

    rw_move = Transfer(range(1, NW), rw_copy)
    rw_move.start()

    forward_tiles(near_first[14:])

    def rows_of(wk):
        return mm.at[pl.ds(pl.multiple_of(wk * WK, WK), WK)]

    def mx_copy(d):
        return to_week(rows_of(w), rows_of(w), mx_s.at[d], mx_r.at[d], x_peer(d))

    def mx_arrived(d):
        return to_week(rows_of(w), rows_of(x_from(d)), mx_s.at[d], mx_r.at[d], x_peer(d))

    def mc_copy(d):
        slot = x_from(d)
        return to_week(rows_of(slot), rows_of(slot), mc_s.at[d], mc_r.at[d], sib)

    def mc_arrived(d):
        slot = x_from(d) + 1 - 2 * core
        return to_week(rows_of(slot), rows_of(slot), mc_s.at[d], mc_r.at[d], sib)

    mx_move = Transfer((1, 3, 2), mx_copy, mx_arrived)
    mc_move = Transfer((0, 1, 3, 2), mc_copy, mc_arrived)
    mx_move.sent += [1, 3, 2]
    mc_move.start((0,))

    rw_move.wait()
    r_sum = r_pack[0]
    for d in range(1, NW):
        r_sum = r_sum + r_week[d]
    r_pack[1] = r_sum

    def rp_copy(d):
        return to_prod(r_pack.at[1], r_prod.at[d], rp_s.at[d], rp_r.at[d], prod_peer(d))

    rp_move = Transfer(range(1, NP), rp_copy)
    rp_move.start()
    for d in (1, 3, 2):
        mx_move.wait((d,))
        mc_move.start((d,))
    wd_move.wait()

    def rest_to_bf16(i):
        d = 1 + i // 2
        slot = chip_from(d) * 2 + lax.rem(i, 2)
        h = 1 - first_half(xi, chip_from(d))
        wb_half(slot, h)[...] = half_of(slot, h)[...].astype(BF16)

    loop(0, NW - 2, rest_to_bf16)

    ba_move.wait()
    lane_all = lax.broadcasted_iota(jnp.int32, (WEEKS, 128), 1)
    pieces = []
    for i in range(NW):
        piece = b_all[i]
        pieces += [piece, pltpu.roll(piece, 64, 1)]
    b = jnp.concatenate(pieces, axis=0)
    wt = jnp.sum(jnp.where(lane_all == K, b, 0.0), axis=1, keepdims=True)
    b = jnp.where(lane_all < K, b, 0.0)
    we1 = b / wt
    weight_total = jnp.sum(wt, axis=0, keepdims=True)

    mc_move.wait()

    def put_m(rows, cols, v):
        hi, mid, lo = split3(v)
        m_hi[rows, cols] = hi
        m_mid[rows, cols] = mid
        m_lo[rows, cols] = lo

    blocks = [slice(a * 128, a * 128 + 128) for a in range(NX)]
    for a in range(NX):
        put_m(blocks[a], blocks[a], mm[blocks[a], blocks[a]])
        for c in range(a + 1, NX):
            both = mm[blocks[a], blocks[c]] + mm[blocks[c], blocks[a]].T
            put_m(blocks[a], blocks[c], both)
            put_m(blocks[c], blocks[a], both.T)

    def apply_m(v):
        hi, mid, lo = [part.astype(F32) for part in split3(v)]
        parts = (hi + pltpu.roll(mid, K, 1) + pltpu.roll(lo, 2 * K, 1)).astype(BF16)
        acc = jnp.dot(m_hi[...], parts, preferred_element_type=F32)
        acc = acc + jnp.where(lane_all < 2 * K, jnp.dot(m_mid[...], parts, preferred_element_type=F32), 0.0)
        acc = acc + jnp.where(lane_all < K, jnp.dot(m_lo[...], parts, preferred_element_type=F32), 0.0)
        acc = acc + (pltpu.roll(acc, 128 - K, 1) + pltpu.roll(acc, 128 - 2 * K, 1))
        return jnp.where(lane_all < K, acc, 0.0)

    n1 = apply_m(we1)
    we2 = (b + n1) / wt
    we3 = (b + apply_m(we2)) / wt
    n3 = apply_m(we3)
    we4 = (b + n3) / wt
    we_buf[...] = we4
    we4_out[...] = we_buf[own_rows, :]

    we3_t = we3.T[:K]
    hi, mid, lo = split3(we3_t)
    rows = jnp.concatenate([hi, mid, lo], axis=0)
    wp3 = lax.dot_general(rows, wb[...], NN, preferred_element_type=F32)
    wp = wp3[:K] + (wp3[K:2 * K] + wp3[2 * K:])
    pe4_out[...] = pe1[...] - wp / pt[...]

    rp_move.wait()
    r_total = lax.fori_loop(1, NP, lambda d, a: a + r_prod[d], r_pack[1])
    gram = lax.dot_general((we3 - we4).T[:K], n3, NN, precision=HI, preferred_element_type=F32)
    gram = gram - lax.dot_general(we3_t, n1, NN, precision=HI, preferred_element_type=F32)
    r_rows = jnp.concatenate(
        [r_total] + [pltpu.roll(r_total, 128 - 32 * a, 1) for a in range(1, 4)], axis=0
    )
    gram_out[...] = ((r_rows + gram) / weight_total)[:, :K]

    for move in (
        pt_move, ps_move, wx_move, wc_move, wy_move, wd_move, pe_move, pf_move, by_move, bz_move, ba_move,
        ms_move, ma_move, mx_move, mc_move, rw_move, rp_move,
    ):
        move.drain()


def effects(x, cell):
    vmem = pl.BlockSpec(memory_space=pltpu.VMEM)
    dma = pltpu.SemaphoreType.DMA
    scratch = [
        pltpu.VMEM((K, WK, PD), BF16),
        pltpu.VMEM((NW, WK, PD), F32),
        pltpu.VMEM((WEEKS, PD), BF16),
        pltpu.VMEM((1, PD), F32),
        pltpu.VMEM((1, PD), F32),
        pltpu.VMEM((NX, 1, PD), F32),
        pltpu.VMEM((1, PD), F32),
        pltpu.VMEM((2, NX, 8, HALF), F32),
        pltpu.VMEM((NX, 8, HALF), F32),
        pltpu.VMEM((NX, 8, HALF), F32),
        pltpu.VMEM((NW, 8, HALF), F32),
        pltpu.VMEM((K, PD), F32),
        pltpu.VMEM((2, 24, 128), F32),
        pltpu.VMEM((4, 24, 128), F32),
        pltpu.VMEM((8, 24, 128), F32),
        pltpu.VMEM((NW, 32, 128), F32),
        pltpu.VMEM((NP, 8, 128), F32),
        pltpu.VMEM((NP, 8, 128), F32),
        pltpu.VMEM((WEEKS, WEEKS), F32),
        pltpu.VMEM((WEEKS, WEEKS), BF16),
        pltpu.VMEM((WEEKS, WEEKS), BF16),
        pltpu.VMEM((WEEKS, WEEKS), BF16),
        pltpu.VMEM((8, K * 8, PD), BF16),
        pltpu.VMEM((8, K * 8, PD), BF16),
        pltpu.VMEM((2, 8, 128), F32),
        pltpu.VMEM((NW, 8, 128), F32),
        pltpu.VMEM((NP, 8, 128), F32),
        pltpu.VMEM((WEEKS, 128), F32),
        dma((4,)),
        pltpu.SemaphoreType.REGULAR,
    ]
    for n in (NX, NX, NX, NX, len(W_PARTS) * NX, len(W_PARTS) * NX, NX, NX, 4, 8, NW, NP, NP, NX, NX, NW, NP):
        scratch += [dma((n,)), dma((n,))]
    return pl.pallas_call(
        effects_kernel,
        out_shape=(
            jax.ShapeDtypeStruct((K, PD), F32),
            jax.ShapeDtypeStruct((WK, 128), F32),
            jax.ShapeDtypeStruct((K, K), F32),
        ),
        in_specs=[pl.BlockSpec(memory_space=pl.ANY), vmem],
        out_specs=(vmem, vmem, vmem),
        scratch_shapes=scratch,
        compiler_params=pltpu.CompilerParams(
            collective_id=0, has_side_effects=True, vmem_limit_bytes=VMEM_LIMIT
        ),
        name="effects",
    )(x, cell)


KB = 4


def output_kernel(x, cell, pe4, we4, gram, out_hbm, gram_out, out, sem):
    gram_out[...] = gram[...]
    lane = lax.broadcasted_iota(jnp.int32, (WK, 128), 1)

    def copy(i):
        rows = pl.ds(i * KB, KB)
        return pltpu.make_async_copy(out.at[rows], out_hbm.at[rows], sem.at[i])

    def block(i):
        for e in range(KB):
            k = i * KB + e
            col = jnp.sum(jnp.where(lane == k, we4[...], 0.0), axis=1, keepdims=True)
            for c in range(PD // LC):
                lanes = slice(c * LC, (c + 1) * LC)
                field = x[k, :, lanes].astype(F32) - pe4[pl.ds(k, 1), lanes] - col
                out[k, :, lanes] = jnp.where(cell[:, lanes] > 0.0, field, 0.0).astype(BF16)
        copy(i).start()

    loop(0, K // KB, block)
    loop(0, K // KB, lambda i: copy(i).wait())


def output(x, cell, pe4, we4, gram):
    vmem = pl.BlockSpec(memory_space=pltpu.VMEM)
    return pl.pallas_call(
        output_kernel,
        out_shape=(
            jax.ShapeDtypeStruct((K, WK, PD), BF16),
            jax.ShapeDtypeStruct((K, K), F32),
        ),
        in_specs=[vmem] * 5,
        out_specs=(pl.BlockSpec(memory_space=pl.ANY), vmem),
        scratch_shapes=[pltpu.VMEM((K, WK, PD), BF16), pltpu.SemaphoreType.DMA((K // KB,))],
        compiler_params=pltpu.CompilerParams(vmem_limit_bytes=32 * 2**20),
        name="output",
    )(x, cell, pe4, we4, gram)


def per_device(regressors, weights, first_week, last_week):
    ids = lax.axis_index("week") * WK + lax.broadcasted_iota(jnp.int32, (WK, PD), 0)
    live = (ids >= first_week[None, :]) & (ids <= last_week[None, :])
    cell = jnp.where(live, weights.astype(F32), 0.0)
    pe4, we4, gram = effects(regressors, cell)
    return output(regressors, cell, pe4, we4, gram)


def solution(mesh):
    return jax.shard_map(
        per_device,
        mesh=mesh,
        in_specs=(P(None, "week", "prod"), P("week", "prod"), P("prod"), P("prod")),
        out_specs=(P(None, "week", "prod"), P()),
        check_vma=False,
    )
```
